32 devices in a mesh: gx: 8 (over z, x), gy: 4 (over y, core).
Axes of the slice: x: 2, y: 2, z: 4, core: 2. Of those that a mesh axis runs over, the one named last changes fastest.
Arguments:
- tracers: float32 [2, 16, 1024, 512], P(None, None, 'gx', 'gy'), may hold values from -6 to 6
- east_flow: bfloat16 [16, 1024, 512], P(None, 'gx', 'gy'), may hold values from -0.14941406 to 0.14941406
- north_flow: bfloat16 [16, 1024, 512], P(None, 'gx', 'gy'), may hold values from -0.14941406 to 0.14941406
- levels: int32 [1024, 512], P('gx', 'gy'), may hold values from 0 to 16, as said below
Outputs:
- new_tracers: float32 [2, 16, 1024, 512], P(None, None, 'gx', 'gy')
- pressure: float32 [1024, 512], P('gx', 'gy')
The draws below stay inside these ranges and needn't reach their ends.
Inputs may be any that keep to these rules, and one draw needn't show every extreme that they name: Land (0) comes in patches, more of it to the east; every ocean column has 1 to 16 levels.
All inputs are finite; a program needn't handle non-finite values.
Results may differ from the reference program's by a relative error of at most 0.0003.
Values may be sent and summed in bfloat16 or wider, within the bound.
A program may use at most 128 MiB of HBM per device.

```python
import jax
import jax.numpy as jnp
from jax import lax

KL = 16
NSTEP = 2
ITERS = 3
NX = 1024
NY = 512


def draw_levels(key, part):
    key = jax.random.fold_in(key, 11)
    coarse_key, depth_key = jax.random.split(key)
    coarse_x = NX // 8
    coarse_y = NY // 8
    column_index = jnp.arange(coarse_x, dtype=jnp.int32)[:, None]
    threshold = 1 + 6 * column_index // coarse_x
    coarse = jax.random.randint(coarse_key, (coarse_x, coarse_y), 0, 8, dtype=jnp.int32)
    land = coarse < threshold
    land = jnp.repeat(jnp.repeat(land, 8, axis=0), 8, axis=1)
    depth = jax.random.randint(depth_key, (NX, NY), 1, KL + 1, dtype=jnp.int32)
    return jnp.where(land, 0, depth).astype(jnp.int32)


def block_levels(own_key, shape, pieces, low, top_value):
    def one(dim, parts):
        steps = jax.random.uniform(jax.random.fold_in(jax.random.fold_in(own_key, 6), dim), (parts,), jnp.float32, low / len(pieces), top_value / len(pieces))
        return jnp.repeat(jnp.exp(steps), shape[dim] // parts).reshape((-1,) + (1,) * (len(shape) - dim - 1))

    level = one(*pieces[0])
    for cut in pieces[1:]:
        level = level * one(*cut)
    return level


def normal_values(own_key, extent, spread, limit, shards=(), kind=jnp.bfloat16):
    array = spread * jax.random.normal(own_key, extent, jnp.float32)
    if shards:
        array = array * block_levels(own_key, extent, shards, -0.22, 0.18)
    return jnp.clip(array, -limit, limit).astype(kind)


def setup_inputs(seed: int = 0) -> dict:
    key_of = jax.random.split(jax.random.key(seed), 5)
    tracers = normal_values(key_of[0], (2, KL, NX, NY), 1.0, 6.0, ((2, 8), (3, 4)), jnp.float32)
    east_flow = jnp.clip(jax.random.uniform(key_of[1], (KL, NX, NY), jnp.float32, -0.14941406, 0.14941406) * block_levels(key_of[1], (KL, NX, NY), ((1, 8), (2, 4)), -0.4, 0.0), -0.14941406, 0.14941406).astype(jnp.bfloat16)
    north_flow = jnp.clip(jax.random.uniform(key_of[2], (KL, NX, NY), jnp.float32, -0.14941406, 0.14941406) * block_levels(key_of[2], (KL, NX, NY), ((1, 8), (2, 4)), -0.4, 0.0), -0.14941406, 0.14941406).astype(jnp.bfloat16)
    levels = draw_levels(jax.random.fold_in(key_of[4], 71), 0)
    return {"tracers": tracers, "east_flow": east_flow, "north_flow": north_flow, "levels": levels}


KAPPA = 0.08
ALPHA = 0.05


def shift_north(field):
    return jnp.concatenate([field[..., 1:], jnp.zeros_like(field[..., :1])], axis=-1)


def shift_south(field):
    return jnp.concatenate([jnp.zeros_like(field[..., :1]), field[..., :-1]], axis=-1)


def level_update(level_index, tracers, east_flow, north_flow, levels):
    column = lax.dynamic_index_in_dim(tracers, level_index, axis=1, keepdims=False)
    east_speed = lax.dynamic_index_in_dim(east_flow, level_index, axis=0, keepdims=False).astype(jnp.float32)
    north_speed = lax.dynamic_index_in_dim(north_flow, level_index, axis=0, keepdims=False).astype(jnp.float32)
    wet = (level_index < levels).astype(jnp.float32)
    open_east = wet * jnp.roll(wet, -1, axis=0)
    open_north = wet * shift_north(wet)
    east_face = east_speed * open_east
    north_face = north_speed * open_north
    for step_index in range(NSTEP):
        east_value = jnp.roll(column, -1, axis=1)
        north_value = shift_north(column)
        east_flux = jnp.maximum(east_face, 0.0) * column + jnp.minimum(east_face, 0.0) * east_value - KAPPA * open_east * (east_value - column)
        north_flux = jnp.maximum(north_face, 0.0) * column + jnp.minimum(north_face, 0.0) * north_value - KAPPA * open_north * (north_value - column)
        column = (column - (east_flux - jnp.roll(east_flux, 1, axis=1)) - (north_flux - shift_south(north_flux))) * wet
    forcing_term = wet * (column[0] - 0.8 * column[1])
    return column, forcing_term


def reference(tracers, east_flow, north_flow, levels):
    def one_level(level_index):
        return level_update(level_index, tracers, east_flow, north_flow, levels)

    columns, terms = lax.map(one_level, jnp.arange(KL, dtype=jnp.int32))
    new_tracers = jnp.moveaxis(columns, 0, 1)
    forcing = 0.25 * jnp.sum(terms, axis=0)
    depth = levels.astype(jnp.float32) / KL
    ocean = (levels > 0).astype(jnp.float32)
    east_coef = jnp.minimum(depth, jnp.roll(depth, -1, axis=0))
    west_coef = jnp.roll(east_coef, 1, axis=0)
    north_coef = jnp.minimum(depth, shift_north(depth))
    south_coef = shift_south(north_coef)
    diagonal = ALPHA * depth + (1.0 - ocean) + east_coef + west_coef + north_coef + south_coef

    def operate(field):
        return diagonal * field - east_coef * jnp.roll(field, -1, axis=0) - west_coef * jnp.roll(field, 1, axis=0) - north_coef * shift_north(field) - south_coef * shift_south(field)

    solution = jnp.zeros_like(forcing)
    residual = forcing
    precond = residual / diagonal
    direction = precond
    rz_now = jnp.sum(residual * precond)
    for step_index in range(ITERS):
        image = operate(direction)
        alpha = rz_now / jnp.sum(direction * image)
        solution = solution + alpha * direction
        residual = residual - alpha * image
        precond = residual / diagonal
        rz_next = jnp.sum(residual * precond)
        direction = precond + (rz_next / rz_now) * direction
        rz_now = rz_next
    return new_tracers, solution
```

```python
import functools

import jax
import jax.numpy as jnp
from jax import lax
from jax.experimental import pallas as pl
from jax.experimental.pallas import tpu as pltpu
from jax.sharding import PartitionSpec as P

MESH = pl.DeviceIdType.MESH
ITERS = 3
KAPPA = 0.08
ALPHA = 0.05
HALO = 8
PIECES = 4


def fused(
    gx, gy,
    tracers, east_flow, north_flow, levels,
    new_tracers, pressure,
    q0, q1, q2, east_raw, north_raw, east_pad, level_block, level_ext,
    coef_c, coef_e, coef_w, coef_n, coef_s, reach, operator_ext,
    row_out_a, row_out_b, row_in_a, row_in_b, side_out, side_in, merged,
    forcing, forcing_ext, gram_y, gram_x,
    load_sem, store_sem, ext_send, ext_recv, near_send, near_recv,
    sum_send, sum_recv,
):
    planes, rows, cols = tracers.shape
    kl = planes // 2
    top = HALO + rows
    ext = rows + 2 * HALO
    mx = lax.axis_index("gx")
    my = lax.axis_index("gy")

    def device(dx, dy):
        return {"gx": lax.rem(mx + dx + gx, gx), "gy": lax.rem(my + dy + gy, gy)}

    loads = [
        pltpu.make_async_copy(levels, level_block, load_sem.at[0]),
        pltpu.make_async_copy(east_flow, east_raw, load_sem.at[1]),
        pltpu.make_async_copy(north_flow, north_raw, load_sem.at[2]),
    ]
    share = planes // PIECES
    for piece in range(PIECES):
        loads.append(
            pltpu.make_async_copy(
                tracers.at[pl.ds(piece * share, share)],
                q0.at[pl.ds(piece * share, share), pl.ds(HALO, rows)],
                load_sem.at[3 + piece],
            )
        )
    for load in loads:
        load.start()

    partners = [(dx, 0) for dx in range(1, gx)] + [(0, dy) for dy in range(1, gy)]
    partners += [(1, 1), (1, -1), (-1, 1), (-1, -1)]
    barrier = pltpu.get_barrier_semaphore()
    for dx, dy in partners:
        pl.semaphore_signal(barrier, inc=1, device_id=device(dx, dy), device_id_type=MESH)

    def ext_copies(block, target, which):
        last, first, whole = pl.ds(rows - HALO, HALO), pl.ds(0, HALO), pl.ds(0, rows)
        low, high, middle = pl.ds(0, HALO), pl.ds(top, HALO), pl.ds(HALO, rows)
        plan = [
            (1, 0, last, 0, low), (-1, 0, first, 0, high),
            (0, 1, whole, 2, middle), (0, -1, whole, 1, middle),
            (1, 1, last, 2, low), (-1, 1, first, 2, high),
            (1, -1, last, 1, low), (-1, -1, first, 1, high),
        ]
        return [
            pltpu.make_async_remote_copy(
                src_ref=block.at[source],
                dst_ref=target.at[slot, place],
                send_sem=ext_send.at[which, n],
                recv_sem=ext_recv.at[which, n],
                device_id=device(dx, dy),
                device_id_type=MESH,
            )
            for n, (dx, dy, source, slot, place) in enumerate(plan)
        ]

    def near_copies(which):
        plan = [
            (1, 0, row_out_a, lambda w: row_in_a.at[w]), (-1, 0, row_out_b, lambda w: row_in_b.at[w]),
            (0, 1, side_out, lambda w: side_in.at[w, 1]), (0, -1, side_out, lambda w: side_in.at[w, 0]),
        ]
        return [
            pltpu.make_async_remote_copy(
                src_ref=source.at[which],
                dst_ref=place(which),
                send_sem=near_send.at[which, n],
                recv_sem=near_recv.at[which, n],
                device_id=device(dx, dy),
                device_id_type=MESH,
            )
            for n, (dx, dy, source, place) in enumerate(plan)
        ]

    lane = lax.broadcasted_iota(jnp.int32, (rows, cols), 1)

    def put_side(which, index, value):
        here = (lane == 2 * index) | (lane == lax.rem(2 * index + cols - 1, cols))
        side_out[which] = jnp.where(here, pltpu.roll(value, 2 * index, 1), side_out[which])

    side_out[...] = jnp.zeros_like(side_out)
    loads[0].wait()
    pl.semaphore_wait(barrier, len(partners))
    level_copies = ext_copies(level_block, level_ext, 0)
    for copy in level_copies:
        copy.start()
    level_ext[0, pl.ds(HALO, rows), :] = level_block[...]

    loads[1].wait()
    loads[2].wait()

    def take_flow(k, carry):
        flow = east_raw[k].astype(jnp.float32)
        east_pad[k, pl.ds(HALO, rows), :] = flow
        put_side(0, planes + k, north_raw[k].astype(jnp.float32))
        return carry

    lax.fori_loop(0, kl, take_flow, 0)
    for load in loads[3:]:
        load.wait()

    def pack(i, carry):
        put_side(0, i, q0[i, pl.ds(HALO, rows), :])
        return carry

    lax.fori_loop(0, planes, pack, 0)

    def rows_out(which, q):
        for i in range(planes):
            row_out_a[which, pl.ds(i, 1), :] = q[i, pl.ds(top - 1, 1), :]
            row_out_b[which, pl.ds(i, 1), :] = q[i, pl.ds(HALO, 1), :]

    def rows_in(which, q):
        for i in range(planes):
            q[i, pl.ds(HALO - 1, 1), :] = row_in_a[which, pl.ds(i, 1), :]
            q[i, pl.ds(top, 1), :] = row_in_b[which, pl.ds(i, 1), :]

    rows_out(0, q0)
    for k in range(kl):
        row_out_a[0, pl.ds(planes + k, 1), :] = east_pad[k, pl.ds(top - 1, 1), :]
    first_copies = near_copies(0)
    for copy in first_copies:
        copy.start()

    for copy in level_copies:
        copy.wait_recv()
    lane_ext = lax.broadcasted_iota(jnp.int32, (ext, cols), 1)

    def join(parts):
        return jnp.concatenate(
            [parts[0], jnp.where(lane_ext < cols // 2, parts[1], parts[2])], axis=1
        )

    def neighbours(value):
        return (
            pltpu.roll(value, ext - 1, 0), pltpu.roll(value, 1, 0),
            pltpu.roll(value, 2 * cols - 1, 1), pltpu.roll(value, 1, 1),
        )

    known_north = (my < gy - 1).astype(jnp.float32)
    known_south = (my > 0).astype(jnp.float32)
    depth = join(
        [
            level_ext[0].astype(jnp.float32),
            level_ext[1].astype(jnp.float32) * known_north,
            level_ext[2].astype(jnp.float32) * known_south,
        ]
    ) / kl
    sides = [jnp.minimum(depth, other) for other in neighbours(depth)]
    diagonal = ALPHA * depth + (depth == 0.0).astype(jnp.float32)
    diagonal = diagonal + sides[0] + sides[1] + sides[2] + sides[3]
    inverse = 1.0 / diagonal
    for n, side in enumerate(sides):
        operator_ext[n] = -side * inverse
        reach[n] = side[HALO:top, :cols] * kl
    operator_ext[4] = diagonal
    operator_ext[5] = inverse
    reach[4] = depth[HALO:top, :cols] * kl

    def merge(which):
        merged[...] = jnp.where(
            lax.rem(lane, 2) == 0, side_in[which, 0], pltpu.roll(side_in[which, 1], 2, 1)
        )

    def halo_of(index):
        return pltpu.roll(merged[...], cols - 1 - 2 * index, 1)

    def advance(q, i, k):
        here = q[i, pl.ds(HALO, rows), :]
        halo = halo_of(i)
        north = jnp.where(lane == cols - 1, halo, pltpu.roll(here, cols - 1, 1))
        south = jnp.where(lane == 0, halo, pltpu.roll(here, 1, 1))
        return (
            coef_c[k] * here
            + coef_e[k] * q[i, pl.ds(HALO + 1, rows), :]
            + coef_w[k] * q[i, pl.ds(HALO - 1, rows), :]
            + coef_n[k] * north
            + coef_s[k] * south
        )

    for copy in first_copies:
        copy.wait_recv()
    rows_in(0, q0)
    for k in range(kl):
        east_pad[k, pl.ds(HALO - 1, 1), :] = row_in_a[0, pl.ds(planes + k, 1), :]
    merge(0)

    def first_step(k, carry):
        level = k.astype(jnp.float32)
        east = east_pad[k, pl.ds(HALO, rows), :]
        west = east_pad[k, pl.ds(HALO - 1, rows), :]
        north = north_raw[k].astype(jnp.float32)
        south = jnp.where(lane == 0, halo_of(planes + k), pltpu.roll(north, 1, 1))

        def gate(n, value):
            return jnp.where(level < reach[n], value, 0.0)

        def out_of(face):
            return jnp.maximum(face, 0.0) + KAPPA

        def back(face):
            return KAPPA - jnp.minimum(face, 0.0)

        coef_e[k] = gate(0, back(east))
        coef_w[k] = gate(1, out_of(west))
        coef_n[k] = gate(2, back(north))
        coef_s[k] = gate(3, out_of(south))
        lost = gate(0, out_of(east)) + gate(1, back(west)) + gate(2, out_of(north)) + gate(3, back(south))
        coef_c[k] = gate(4, 1.0 - lost)
        for tracer in range(2):
            i = tracer * kl + k
            value = advance(q0, i, k)
            q1[i, pl.ds(HALO, rows), :] = value
            put_side(1, i, value)
        return carry

    lax.fori_loop(0, kl, first_step, 0)
    rows_out(1, q1)
    second_copies = near_copies(1)
    for copy in second_copies:
        copy.start()
    forcing[...] = jnp.zeros_like(forcing)
    for copy in second_copies:
        copy.wait_recv()
    rows_in(1, q1)
    merge(1)

    def second_step(k, carry):
        heat = advance(q1, k, k)
        salt = advance(q1, kl + k, k)
        q2[k] = heat
        q2[kl + k] = salt
        forcing[...] += 0.25 * (heat - 0.8 * salt)
        return carry

    lax.fori_loop(0, kl, second_step, 0)
    stores = []
    for piece in range(PIECES):
        part = pl.ds(piece * share, share)
        stores.append(pltpu.make_async_copy(q2.at[part], new_tracers.at[part], store_sem.at[piece]))

    forcing_copies = ext_copies(forcing, forcing_ext, 1)
    for copy in forcing_copies:
        copy.start()
    for store in stores:
        store.start()
    forcing_ext[0, pl.ds(HALO, rows), :] = forcing[...]
    for copy in forcing_copies:
        copy.wait_recv()
    basis = [join([forcing_ext[0], forcing_ext[1], forcing_ext[2]]) * operator_ext[5]]
    for step in range(ITERS):
        others = neighbours(basis[-1])
        basis.append(sum(operator_ext[n] * others[n] for n in range(4)))
    basis = [vector[HALO:top, :cols] for vector in basis]
    own_diagonal = operator_ext[4, pl.ds(HALO, rows), pl.ds(0, cols)]
    scaled = [own_diagonal * vector for vector in basis[:ITERS]]
    gram_y[0] = jnp.zeros_like(gram_y[0])
    for n in range(2 * ITERS):
        product = scaled[n // 2] * basis[(n + 1) // 2]
        gram_y[0, pl.ds(n, 1), :] = jnp.sum(product, axis=0, keepdims=True)

    def spread(buffer, count, place, axis):
        copies = []
        for step in range(1, count):
            copies.append(
                pltpu.make_async_remote_copy(
                    src_ref=buffer.at[0],
                    dst_ref=buffer.at[step],
                    send_sem=sum_send.at[axis, step],
                    recv_sem=sum_recv.at[axis, step],
                    device_id=place(step),
                    device_id_type=MESH,
                )
            )
        for copy in copies:
            copy.start()
        for copy in copies:
            copy.wait_recv()
        return copies

    y_copies = spread(gram_y, gy, lambda step: device(0, step), 0)
    gram_x[0] = jnp.sum(gram_y[...], axis=0)
    x_copies = spread(gram_x, gx, lambda step: device(step, 0), 1)
    total = jnp.sum(jnp.sum(gram_x[...], axis=0), axis=1, keepdims=True)
    moment = [total[n : n + 1, :] for n in range(2 * ITERS)]

    def inner(left, right):
        terms = [
            a * b * moment[i + j]
            for i, a in enumerate(left) for j, b in enumerate(right)
        ]
        return functools.reduce(lambda x, y: x + y, terms)

    def applied(poly):
        grown = poly + [jnp.zeros_like(poly[0])]
        return [grown[0]] + [grown[n] + grown[n - 1] for n in range(1, len(grown))]

    one = jnp.ones_like(moment[0])
    precond, direction, answer = [one], [one], []
    rz_now = inner(precond, precond)
    for step in range(ITERS):
        image = applied(direction)
        alpha = rz_now / inner(direction, image)
        answer = [
            (answer[n] if n < len(answer) else 0.0) + alpha * direction[n]
            for n in range(len(direction))
        ]
        if step + 1 < ITERS:
            precond = [
                (precond[n] if n < len(precond) else 0.0) - alpha * image[n]
                for n in range(len(image))
            ]
            rz_next = inner(precond, precond)
            beta = rz_next / rz_now
            direction = [
                precond[n] + (beta * direction[n] if n < len(direction) else 0.0)
                for n in range(len(precond))
            ]
            rz_now = rz_next
    pressure[...] = answer[0] * basis[0] + answer[1] * basis[1] + answer[2] * basis[2]

    for copy in level_copies + first_copies + second_copies + forcing_copies + y_copies + x_copies:
        copy.wait_send()
    for store in stores:
        store.wait()


def on_device(gx, gy, tracers, east_flow, north_flow, levels):
    pair, kl, rows, cols = tracers.shape
    planes = pair * kl
    ext = rows + 2 * HALO
    f32 = jnp.float32
    any_space = pl.BlockSpec(memory_space=pl.ANY)
    plane = (kl, rows, cols)
    packed_rows = planes + kl
    new_tracers, pressure = pl.pallas_call(
        functools.partial(fused, gx, gy),
        out_shape=(
            jax.ShapeDtypeStruct((planes, rows, cols), f32),
            jax.ShapeDtypeStruct((rows, cols), f32),
        ),
        in_specs=[any_space] * 4,
        out_specs=(any_space, pl.BlockSpec(memory_space=pltpu.VMEM)),
        scratch_shapes=[
            pltpu.VMEM((planes, ext, cols), f32),
            pltpu.VMEM((planes, ext, cols), f32),
            pltpu.VMEM((planes, rows, cols), f32),
            pltpu.VMEM(plane, jnp.bfloat16),
            pltpu.VMEM(plane, jnp.bfloat16),
            pltpu.VMEM((kl, HALO + rows, cols), f32),
            pltpu.VMEM((rows, cols), jnp.int32),
            pltpu.VMEM((3, ext, cols), jnp.int32),
            pltpu.VMEM(plane, f32),
            pltpu.VMEM(plane, f32),
            pltpu.VMEM(plane, f32),
            pltpu.VMEM(plane, f32),
            pltpu.VMEM(plane, f32),
            pltpu.VMEM((5, rows, cols), f32),
            pltpu.VMEM((6, ext, 2 * cols), f32),
            pltpu.VMEM((2, packed_rows, cols), f32),
            pltpu.VMEM((2, packed_rows, cols), f32),
            pltpu.VMEM((2, packed_rows, cols), f32),
            pltpu.VMEM((2, packed_rows, cols), f32),
            pltpu.VMEM((2, rows, cols), f32),
            pltpu.VMEM((2, 2, rows, cols), f32),
            pltpu.VMEM((rows, cols), f32),
            pltpu.VMEM((rows, cols), f32),
            pltpu.VMEM((3, ext, cols), f32),
            pltpu.VMEM((gy, 8, cols), f32),
            pltpu.VMEM((gx, 8, cols), f32),
            pltpu.SemaphoreType.DMA((3 + PIECES,)),
            pltpu.SemaphoreType.DMA((PIECES,)),
            pltpu.SemaphoreType.DMA((2, 8)),
            pltpu.SemaphoreType.DMA((2, 8)),
            pltpu.SemaphoreType.DMA((2, 4)),
            pltpu.SemaphoreType.DMA((2, 4)),
            pltpu.SemaphoreType.DMA((2, max(gx, gy))),
            pltpu.SemaphoreType.DMA((2, max(gx, gy))),
        ],
        compiler_params=pltpu.CompilerParams(
            collective_id=0, has_side_effects=True, vmem_limit_bytes=48 * 1024 * 1024
        ),
    )(tracers.reshape(planes, rows, cols), east_flow, north_flow, levels)
    return new_tracers.reshape(tracers.shape), pressure


def solution(mesh):
    placed = (P(None, None, "gx", "gy"), P(None, "gx", "gy"), P(None, "gx", "gy"), P("gx", "gy"))
    return jax.shard_map(
        functools.partial(on_device, mesh.shape["gx"], mesh.shape["gy"]),
        mesh=mesh,
        in_specs=placed,
        out_specs=(P(None, None, "gx", "gy"), P("gx", "gy")),
        check_vma=False,
    )
```

```python
import functools

import jax
import jax.numpy as jnp
from jax import lax
from jax.experimental import pallas as pl
from jax.experimental.pallas import tpu as pltpu
from jax.sharding import PartitionSpec as P

MESH = pl.DeviceIdType.MESH
ITERS = 3
KAPPA = 0.08
ALPHA = 0.05
HALO = 8
PAD = 16
PIECES = 4


def fused(
    gx, gy,
    tracers, east_flow, north_flow, levels,
    new_tracers, pressure,
    q0, q1, q2, east_raw, north_raw, east_pad, north_pad, level_block, level_ext,
    coef_c, coef_e, coef_w, coef_n, coef_s, reach, side_reach, operator_ext,
    flow_out, flow_in, row_out, row_in, flow_side, q_side, flow_join, east_join, q_join, q_swap,
    forcing_ext, gram_y, gram_x,
    load_sem, store_sem, ext_send, ext_recv, row_send, row_recv,
    sum_send, sum_recv,
):
    planes, rows, cols = tracers.shape
    kl = planes // 2
    top = HALO + rows
    ext = rows + 2 * HALO
    mx = lax.axis_index("gx")
    my = lax.axis_index("gy")
    own = pl.ds(HALO, rows)

    def device(dx, dy):
        return {"gx": lax.rem(mx + dx + gx, gx), "gy": lax.rem(my + dy + gy, gy)}

    loads = [
        pltpu.make_async_copy(levels, level_block, load_sem.at[0]),
        pltpu.make_async_copy(east_flow, east_raw, load_sem.at[1]),
        pltpu.make_async_copy(north_flow, north_raw, load_sem.at[2]),
    ]
    share = planes // PIECES
    for piece in range(PIECES):
        loads.append(
            pltpu.make_async_copy(
                tracers.at[pl.ds(piece * share, share)],
                q0.at[pl.ds(piece * share, share), pl.ds(PAD, rows)],
                load_sem.at[3 + piece],
            )
        )
    for load in loads:
        load.start()

    partners = [(dx, 0) for dx in range(1, gx)] + [(0, dy) for dy in range(1, gy)]
    partners += [(1, 1), (1, -1), (-1, 1), (-1, -1)]
    barrier = pltpu.get_barrier_semaphore()
    for dx, dy in partners:
        pl.semaphore_signal(barrier, inc=1, device_id=device(dx, dy), device_id_type=MESH)

    has_north = my < gy - 1
    has_south = my > 0

    class Exchange:
        def __init__(self, buffer, which, rim, zonal=True):
            last, first, whole = pl.ds(rows, rim), pl.ds(rim, rim), pl.ds(rim, rows)
            low, high = pl.ds(0, rim), pl.ds(rim + rows, rim)
            plan = [
                (0, 1, whole, 2, whole), (0, -1, whole, 1, whole),
                (1, 1, last, 2, low), (-1, 1, first, 2, high),
                (1, -1, last, 1, low), (-1, -1, first, 1, high),
            ]
            if zonal:
                plan += [(1, 0, last, 0, low), (-1, 0, first, 0, high)]
            self.copies = [
                (
                    dy,
                    pltpu.make_async_remote_copy(
                        src_ref=buffer.at[0, source],
                        dst_ref=buffer.at[slot, place],
                        send_sem=ext_send.at[which, n],
                        recv_sem=ext_recv.at[which, n],
                        device_id=device(dx, dy),
                        device_id_type=MESH,
                    ),
                )
                for n, (dx, dy, source, slot, place) in enumerate(plan)
            ]

        def each(self, outward, action):
            for dy, copy in self.copies:
                if dy == 0:
                    action(copy)
                else:
                    pl.when(has_north if (dy > 0) == outward else has_south)(
                        functools.partial(action, copy)
                    )

        def start(self):
            self.each(True, lambda copy: copy.start())

        def wait_recv(self):
            self.each(False, lambda copy: copy.wait_recv())

        def wait_send(self):
            self.each(True, lambda copy: copy.wait_send())

    def row_copies(source, place, which):
        return [
            pltpu.make_async_remote_copy(
                src_ref=source.at[n],
                dst_ref=place.at[n],
                send_sem=row_send.at[which, n],
                recv_sem=row_recv.at[which, n],
                device_id=device(1 - 2 * n, 0),
                device_id_type=MESH,
            )
            for n in range(2)
        ]

    def lanes(count):
        return lax.broadcasted_iota(jnp.int32, (count, cols), 1)

    def rows_out(source, target, base, count):
        for i in range(count):
            target[0, pl.ds(base + 2 * i, 2), :] = source[i, pl.ds(PAD + rows - 2, 2), :]
            target[1, pl.ds(base + 2 * i, 2), :] = source[i, pl.ds(PAD, 2), :]

    def rows_in(source, target, base, count):
        for i in range(count):
            target[i, pl.ds(PAD - 2, 2), :] = source[0, pl.ds(base + 2 * i, 2), :]
            target[i, pl.ds(PAD + rows, 2), :] = source[1, pl.ds(base + 2 * i, 2), :]

    span = 32
    group = lanes(span) >> 2

    def put_side(target, r, pieces):
        place = pl.ds(HALO + r, span)
        total = target[0, place, :]
        for index, value in pieces:
            total = jnp.where(group == index, pltpu.roll(value, 4 * index + 2, 1), total)
        target[0, place, :] = total

    loads[0].wait()
    level_ext[0, pl.ds(PAD, rows), :] = level_block[...].astype(jnp.float32).astype(jnp.bfloat16)
    flow_side[0] = jnp.zeros_like(flow_side[0])
    q_side[0] = jnp.zeros_like(q_side[0])
    loads[1].wait()
    loads[2].wait()

    def take_flow(k, carry):
        for r in range(0, rows, span):
            east = east_raw[k, pl.ds(r, span), :].astype(jnp.float32)
            north = north_raw[k, pl.ds(r, span), :].astype(jnp.float32)
            east_pad[k, pl.ds(PAD + r, span), :] = east
            north_pad[k, pl.ds(PAD + r, span), :] = north
            put_side(flow_side, r, [(k, east), (kl + k, north)])
        return carry

    lax.fori_loop(0, kl, take_flow, 0)
    rows_out(east_pad, flow_out, 0, kl)
    rows_out(north_pad, flow_out, 2 * kl, kl)
    pl.semaphore_wait(barrier, len(partners))
    level_copies = Exchange(level_ext, 0, PAD)
    flow_copies = Exchange(flow_side, 1, HALO, zonal=False)
    q_copies = Exchange(q_side, 2, HALO, zonal=False)
    forcing_copies = Exchange(forcing_ext, 3, HALO)
    flow_rows = row_copies(flow_out, flow_in, 0)
    q_rows = row_copies(row_out, row_in, 1)
    level_copies.start()
    flow_copies.start()
    for copy in flow_rows:
        copy.start()

    for load in loads[3:]:
        load.wait()
    bunch = 4

    def pack(g, carry):
        for r in range(0, rows, span):
            pieces = []
            for j in range(bunch):
                i = g * bunch + j
                pieces.append((i, q0[i, pl.ds(PAD + r, span), :]))
            put_side(q_side, r, pieces)
        return carry

    lax.fori_loop(0, planes // bunch, pack, 0)
    q_copies.start()
    rows_out(q0, row_out, 0, planes)
    for copy in q_rows:
        copy.start()

    level_copies.wait_recv()
    lane_ext = lanes(ext)
    north_lanes = jnp.where(has_north, cols, 0)
    south_lanes = jnp.where(has_south, cols, 0)

    def known(north, south, lane):
        return (
            jnp.where(lane < north_lanes, north, 0.0),
            jnp.where(lane < south_lanes, south, 0.0),
        )

    def join(parts):
        north, south = known(parts[1], parts[2], lane_ext)
        return jnp.concatenate(
            [parts[0], jnp.where(lane_ext < cols // 2, north, south)], axis=1
        )

    def neighbours(value):
        return (
            pltpu.roll(value, ext - 1, 0), pltpu.roll(value, 1, 0),
            pltpu.roll(value, 2 * cols - 1, 1), pltpu.roll(value, 1, 1),
        )

    trim = PAD - HALO
    depth = join(
        [level_ext[n].astype(jnp.float32)[trim : trim + ext] for n in range(3)]
    ) / kl
    sides = [jnp.minimum(depth, other) for other in neighbours(depth)]
    diagonal = ALPHA * depth + (depth == 0.0).astype(jnp.float32)
    diagonal = diagonal + sides[0] + sides[1] + sides[2] + sides[3]
    inverse = 1.0 / diagonal
    lane = lanes(rows)
    corner = lane & 3
    for n, side in enumerate(sides + [depth]):
        if n < 4:
            operator_ext[n] = -side * inverse
        scaled_side = side * kl
        reach[n] = scaled_side[:, :cols]
        edge = scaled_side[HALO:top, cols:]
        side_reach[n] = jnp.where(corner == 1, edge[:, cols - 1 : cols], edge[:, :1])
    operator_ext[4] = diagonal
    operator_ext[5] = inverse

    def merge(side):
        north, south = known(side[1], side[2], lane_ext)
        return jnp.where((lane_ext & 3) >= 2, north, south)

    def coefficients(level, limit, east, west, north, south):
        def gate(n, value):
            return jnp.where(level < limit(n), value, 0.0)

        def out_of(face):
            return jnp.maximum(face, 0.0) + KAPPA

        def back(face):
            return KAPPA - jnp.minimum(face, 0.0)

        lost = gate(0, out_of(east)) + gate(1, back(west)) + gate(2, out_of(north)) + gate(3, back(south))
        return (
            gate(4, 1.0 - lost), gate(0, back(east)), gate(1, out_of(west)),
            gate(2, back(north)), gate(3, out_of(south)),
        )

    flow_copies.wait_recv()
    for copy in flow_rows:
        copy.wait_recv()
    rows_in(flow_in, east_pad, 0, kl)
    rows_in(flow_in, north_pad, 2 * kl, kl)
    flow_join[...] = merge(flow_side)
    wide = 24
    lane_wide = lanes(wide)

    def prepare(k, carry):
        level = k.astype(jnp.float32)
        for e in range(0, ext, wide):
            part = pl.ds(e, wide)
            east = east_pad[k, pl.ds(HALO + e, wide), :]
            west = east_pad[k, pl.ds(HALO + e - 1, wide), :]
            north = north_pad[k, pl.ds(HALO + e, wide), :]
            halo = pltpu.roll(flow_join[part, :], cols // 2 - 1 - 4 * k, 1)
            south = jnp.where(lane_wide == 0, halo, pltpu.roll(north, 1, 1))
            result = coefficients(level, lambda n: reach[n, part, :], east, west, north, south)
            for ref, value in zip((coef_c, coef_e, coef_w, coef_n, coef_s), result):
                ref[k, part, :] = value
        return carry

    lax.fori_loop(0, kl, prepare, 0)

    half = cols // 2
    joined = flow_join[...]
    turned = pltpu.roll(joined, half, 1)
    east_join[...] = jnp.where(lane_ext < half, joined, turned)
    north_side = jnp.where(lane_ext < half, turned, joined)[HALO:top]
    own_flow = flow_side[0, own, :]
    own_north = jnp.where(lane < half, pltpu.roll(own_flow, half, 1), own_flow)
    south_side = jnp.where(corner == 2, pltpu.roll(own_north, 1, 1), pltpu.roll(north_side, 1, 1))
    side_level = ((lane & (half - 1)) >> 2).astype(jnp.float32)
    side_coef = coefficients(
        side_level, lambda n: side_reach[n],
        east_join[own, :], east_join[pl.ds(HALO - 1, rows), :], north_side, south_side,
    )
    q_copies.wait_recv()
    q_join[...] = merge(q_side)
    here = q_join[own, :]
    own_side = q_side[0, own, :]
    north = jnp.where(corner == 1, pltpu.roll(own_side, cols - 1, 1), pltpu.roll(here, cols - 1, 1))
    south = jnp.where(corner == 2, pltpu.roll(own_side, 1, 1), pltpu.roll(here, 1, 1))
    moved = (
        side_coef[0] * here
        + side_coef[1] * q_join[pl.ds(HALO + 1, rows), :]
        + side_coef[2] * q_join[pl.ds(HALO - 1, rows), :]
        + side_coef[3] * north
        + side_coef[4] * south
    )

    def swap(value, place):
        return jnp.where((place & 3) == 1, pltpu.roll(value, cols - 1, 1), pltpu.roll(value, 1, 1))

    q_swap[0] = swap(q_join[...], lane_ext)
    q_swap[1, own, :] = swap(moved, lane)

    for copy in q_rows:
        copy.wait_recv()
    rows_in(row_in, q0, 0, planes)

    def advance(q, which, i, k, e, count, lane_here):
        part = pl.ds(e, count)
        here = q[i, pl.ds(HALO + e, count), :]
        halo = pltpu.roll(q_swap[which, part, :], cols - 2 - 4 * i, 1)
        north = jnp.where(lane_here == cols - 1, halo, pltpu.roll(here, cols - 1, 1))
        south = jnp.where(lane_here == 0, halo, pltpu.roll(here, 1, 1))
        return (
            coef_c[k, part, :] * here
            + coef_e[k, part, :] * q[i, pl.ds(HALO + e + 1, count), :]
            + coef_w[k, part, :] * q[i, pl.ds(HALO + e - 1, count), :]
            + coef_n[k, part, :] * north
            + coef_s[k, part, :] * south
        )

    def first_step(k, carry):
        for e in range(0, ext, wide):
            for tracer in range(2):
                i = tracer * kl + k
                q1[i, pl.ds(HALO + e, wide), :] = advance(q0, 0, i, k, e, wide, lane_wide)
        return carry

    lax.fori_loop(0, kl, first_step, 0)
    forcing_ext[0, own, :] = jnp.zeros((rows, cols), jnp.float32)
    lane_span = lanes(span)

    def second_step(k, carry):
        for r in range(0, rows, span):
            heat = advance(q1, 1, k, k, HALO + r, span, lane_span)
            salt = advance(q1, 1, kl + k, k, HALO + r, span, lane_span)
            q2[k, pl.ds(r, span), :] = heat
            q2[kl + k, pl.ds(r, span), :] = salt
            forcing_ext[0, pl.ds(HALO + r, span), :] += 0.25 * (heat - 0.8 * salt)
        return carry

    lax.fori_loop(0, kl, second_step, 0)
    forcing_copies.start()
    stores = []
    for piece in range(PIECES):
        part = pl.ds(piece * share, share)
        stores.append(pltpu.make_async_copy(q2.at[part], new_tracers.at[part], store_sem.at[piece]))
    for store in stores:
        store.start()

    forcing_copies.wait_recv()
    basis = [join([forcing_ext[0], forcing_ext[1], forcing_ext[2]]) * operator_ext[5]]
    for step in range(ITERS):
        others = neighbours(basis[-1])
        basis.append(sum(operator_ext[n] * others[n] for n in range(4)))
    basis = [vector[HALO:top, :cols] for vector in basis]
    own_diagonal = operator_ext[4, pl.ds(HALO, rows), pl.ds(0, cols)]
    scaled = [own_diagonal * vector for vector in basis[:ITERS]]
    gram_y[0] = jnp.zeros_like(gram_y[0])
    for n in range(2 * ITERS):
        product = scaled[n // 2] * basis[(n + 1) // 2]
        gram_y[0, pl.ds(n, 1), :] = jnp.sum(product, axis=0, keepdims=True)

    def spread(buffer, count, place, axis):
        copies = []
        for step in range(1, count):
            copies.append(
                pltpu.make_async_remote_copy(
                    src_ref=buffer.at[0],
                    dst_ref=buffer.at[step],
                    send_sem=sum_send.at[axis, step],
                    recv_sem=sum_recv.at[axis, step],
                    device_id=place(step),
                    device_id_type=MESH,
                )
            )
        for copy in copies:
            copy.start()
        for copy in copies:
            copy.wait_recv()
        return copies

    y_copies = spread(gram_y, gy, lambda step: device(0, step), 0)
    gram_x[0] = jnp.sum(gram_y[...], axis=0)
    x_copies = spread(gram_x, gx, lambda step: device(step, 0), 1)
    total = jnp.sum(jnp.sum(gram_x[...], axis=0), axis=1, keepdims=True)
    moment = [total[n : n + 1, :] for n in range(2 * ITERS)]

    def inner(left, right):
        terms = [
            a * b * moment[i + j]
            for i, a in enumerate(left) for j, b in enumerate(right)
        ]
        return functools.reduce(lambda x, y: x + y, terms)

    def applied(poly):
        grown = poly + [jnp.zeros_like(poly[0])]
        return [grown[0]] + [grown[n] + grown[n - 1] for n in range(1, len(grown))]

    one = jnp.ones_like(moment[0])
    precond, direction, answer = [one], [one], []
    rz_now = inner(precond, precond)
    for step in range(ITERS):
        image = applied(direction)
        alpha = rz_now / inner(direction, image)
        answer = [
            (answer[n] if n < len(answer) else 0.0) + alpha * direction[n]
            for n in range(len(direction))
        ]
        if step + 1 < ITERS:
            precond = [
                (precond[n] if n < len(precond) else 0.0) - alpha * image[n]
                for n in range(len(image))
            ]
            rz_next = inner(precond, precond)
            beta = rz_next / rz_now
            direction = [
                precond[n] + (beta * direction[n] if n < len(direction) else 0.0)
                for n in range(len(precond))
            ]
            rz_now = rz_next
    pressure[...] = answer[0] * basis[0] + answer[1] * basis[1] + answer[2] * basis[2]

    for exchange in (level_copies, flow_copies, q_copies, forcing_copies):
        exchange.wait_send()
    for copy in flow_rows + q_rows + y_copies + x_copies:
        copy.wait_send()
    for store in stores:
        store.wait()


def on_device(gx, gy, tracers, east_flow, north_flow, levels):
    pair, kl, rows, cols = tracers.shape
    planes = pair * kl
    ext = rows + 2 * HALO
    pad = rows + 2 * PAD
    f32 = jnp.float32
    in_hbm = pl.BlockSpec(memory_space=pltpu.HBM)
    plane = (kl, rows, cols)
    wide_plane = (kl, ext, cols)
    new_tracers, pressure = pl.pallas_call(
        functools.partial(fused, gx, gy),
        out_shape=(
            jax.ShapeDtypeStruct((planes, rows, cols), f32),
            jax.ShapeDtypeStruct((rows, cols), f32),
        ),
        in_specs=[in_hbm] * 4,
        out_specs=(in_hbm, pl.BlockSpec(memory_space=pltpu.VMEM)),
        scratch_shapes=[
            pltpu.VMEM((planes, pad, cols), f32),
            pltpu.VMEM((planes, pad, cols), f32),
            pltpu.VMEM((planes, rows, cols), f32),
            pltpu.VMEM(plane, jnp.bfloat16),
            pltpu.VMEM(plane, jnp.bfloat16),
            pltpu.VMEM((kl, pad, cols), f32),
            pltpu.VMEM((kl, pad, cols), f32),
            pltpu.VMEM((rows, cols), jnp.int32),
            pltpu.VMEM((3, pad, cols), jnp.bfloat16),
            pltpu.VMEM(wide_plane, f32),
            pltpu.VMEM(wide_plane, f32),
            pltpu.VMEM(wide_plane, f32),
            pltpu.VMEM(wide_plane, f32),
            pltpu.VMEM(wide_plane, f32),
            pltpu.VMEM((5, ext, cols), f32),
            pltpu.VMEM((5, rows, cols), f32),
            pltpu.VMEM((6, ext, 2 * cols), f32),
            pltpu.VMEM((2, 4 * kl, cols), f32),
            pltpu.VMEM((2, 4 * kl, cols), f32),
            pltpu.VMEM((2, 2 * planes, cols), f32),
            pltpu.VMEM((2, 2 * planes, cols), f32),
            pltpu.VMEM((3, ext, cols), f32),
            pltpu.VMEM((3, ext, cols), f32),
            pltpu.VMEM((ext, cols), f32),
            pltpu.VMEM((ext, cols), f32),
            pltpu.VMEM((ext, cols), f32),
            pltpu.VMEM((2, ext, cols), f32),
            pltpu.VMEM((3, ext, cols), f32),
            pltpu.VMEM((gy, 8, cols), f32),
            pltpu.VMEM((gx, 8, cols), f32),
            pltpu.SemaphoreType.DMA((3 + PIECES,)),
            pltpu.SemaphoreType.DMA((PIECES,)),
            pltpu.SemaphoreType.DMA((4, 8)),
            pltpu.SemaphoreType.DMA((4, 8)),
            pltpu.SemaphoreType.DMA((2, 2)),
            pltpu.SemaphoreType.DMA((2, 2)),
            pltpu.SemaphoreType.DMA((2, max(gx, gy))),
            pltpu.SemaphoreType.DMA((2, max(gx, gy))),
        ],
        compiler_params=pltpu.CompilerParams(
            collective_id=0, has_side_effects=True, vmem_limit_bytes=60 * 1024 * 1024
        ),
    )(tracers.reshape(planes, rows, cols), east_flow, north_flow, levels)
    return new_tracers.reshape(tracers.shape), pressure


def solution(mesh):
    placed = (P(None, None, "gx", "gy"), P(None, "gx", "gy"), P(None, "gx", "gy"), P("gx", "gy"))
    return jax.shard_map(
        functools.partial(on_device, mesh.shape["gx"], mesh.shape["gy"]),
        mesh=mesh,
        in_specs=placed,
        out_specs=(P(None, None, "gx", "gy"), P("gx", "gy")),
        check_vma=False,
    )
```

```python
import functools

import jax
import jax.numpy as jnp
from jax import lax
from jax.experimental import pallas as pl
from jax.experimental.pallas import tpu as pltpu
from jax.sharding import PartitionSpec as P

MESH = pl.DeviceIdType.MESH
ITERS = 3
KAPPA = 0.08
ALPHA = 0.05
HALO = 8
PAD = 16
PIECES = 4


def fused(
    gx, gy,
    tracers, east_flow, north_flow, levels,
    q2, pressure,
    q0, q1, east_raw, north_raw, east_pad, north_pad, level_block, level_ext,
    coef_c, coef_e, coef_w, coef_n, coef_s, reach, side_reach, operator_ext,
    flow_out, flow_in, row_out, row_in, flow_side, q_side, flow_join, east_join, q_join, q_swap,
    forcing_ext, gram_tile, gram,
    load_sem, ext_send, ext_recv, row_send, row_recv,
    sum_send, sum_recv,
):
    planes, rows, cols = tracers.shape
    kl = planes // 2
    top = HALO + rows
    ext = rows + 2 * HALO
    mx = lax.axis_index("gx")
    my = lax.axis_index("gy")
    own = pl.ds(HALO, rows)

    def device(dx, dy):
        return {"gx": lax.rem(mx + dx + gx, gx), "gy": lax.rem(my + dy + gy, gy)}

    loads = [
        pltpu.make_async_copy(levels, level_block, load_sem.at[0]),
        pltpu.make_async_copy(east_flow, east_raw, load_sem.at[1]),
        pltpu.make_async_copy(north_flow, north_raw, load_sem.at[2]),
    ]
    share = planes // PIECES
    for piece in range(PIECES):
        loads.append(
            pltpu.make_async_copy(
                tracers.at[pl.ds(piece * share, share)],
                q0.at[pl.ds(piece * share, share), pl.ds(PAD, rows)],
                load_sem.at[3 + piece],
            )
        )
    for load in loads:
        load.start()

    others = [(dx, dy) for dx in range(gx) for dy in range(gy) if (dx, dy) != (0, 0)]
    barrier = pltpu.get_barrier_semaphore()
    for dx, dy in others:
        pl.semaphore_signal(barrier, inc=1, device_id=device(dx, dy), device_id_type=MESH)

    has_north = my < gy - 1
    has_south = my > 0

    class Exchange:
        def __init__(self, buffer, which, rim, zonal=True):
            last, first, whole = pl.ds(rows, rim), pl.ds(rim, rim), pl.ds(rim, rows)
            low, high = pl.ds(0, rim), pl.ds(rim + rows, rim)
            plan = [
                (0, 1, whole, 2, whole), (0, -1, whole, 1, whole),
                (1, 1, last, 2, low), (-1, 1, first, 2, high),
                (1, -1, last, 1, low), (-1, -1, first, 1, high),
            ]
            if zonal:
                plan += [(1, 0, last, 0, low), (-1, 0, first, 0, high)]
            self.copies = [
                (
                    dy,
                    pltpu.make_async_remote_copy(
                        src_ref=buffer.at[0, source],
                        dst_ref=buffer.at[slot, place],
                        send_sem=ext_send.at[which, n],
                        recv_sem=ext_recv.at[which, n],
                        device_id=device(dx, dy),
                        device_id_type=MESH,
                    ),
                )
                for n, (dx, dy, source, slot, place) in enumerate(plan)
            ]

        def each(self, outward, action):
            for dy, copy in self.copies:
                if dy == 0:
                    action(copy)
                else:
                    pl.when(has_north if (dy > 0) == outward else has_south)(
                        functools.partial(action, copy)
                    )

        def start(self):
            self.each(True, lambda copy: copy.start())

        def wait_recv(self):
            self.each(False, lambda copy: copy.wait_recv())

        def wait_send(self):
            self.each(True, lambda copy: copy.wait_send())

    def row_copies(source, place, which):
        return [
            pltpu.make_async_remote_copy(
                src_ref=source.at[n],
                dst_ref=place.at[n],
                send_sem=row_send.at[which, n],
                recv_sem=row_recv.at[which, n],
                device_id=device(1 - 2 * n, 0),
                device_id_type=MESH,
            )
            for n in range(2)
        ]

    def lanes(count):
        return lax.broadcasted_iota(jnp.int32, (count, cols), 1)

    def rows_out(source, target, base, count):
        for i in range(count):
            target[0, pl.ds(base + 2 * i, 2), :] = source[i, pl.ds(PAD + rows - 2, 2), :]
            target[1, pl.ds(base + 2 * i, 2), :] = source[i, pl.ds(PAD, 2), :]

    def rows_in(source, target, base, count):
        for i in range(count):
            target[i, pl.ds(PAD - 2, 2), :] = source[0, pl.ds(base + 2 * i, 2), :]
            target[i, pl.ds(PAD + rows, 2), :] = source[1, pl.ds(base + 2 * i, 2), :]

    span = 64
    group = lanes(span) >> 2

    def put_side(target, r, pieces):
        place = pl.ds(HALO + r, span)
        total = target[0, place, :]
        for index, value in pieces:
            total = jnp.where(group == index, pltpu.roll(value, 4 * index + 2, 1), total)
        target[0, place, :] = total

    level_copies = Exchange(level_ext, 0, PAD)
    flow_copies = Exchange(flow_side, 1, HALO, zonal=False)
    q_copies = Exchange(q_side, 2, HALO, zonal=False)
    forcing_copies = Exchange(forcing_ext, 3, HALO)
    flow_rows = row_copies(flow_out, flow_in, 0)
    q_rows = row_copies(row_out, row_in, 1)
    flow_side[0] = jnp.zeros_like(flow_side[0])
    q_side[0] = jnp.zeros_like(q_side[0])
    loads[0].wait()
    level_ext[0, pl.ds(PAD, rows), :] = level_block[...].astype(jnp.float32).astype(jnp.bfloat16)
    pl.semaphore_wait(barrier, len(others))
    level_copies.start()
    loads[1].wait()
    loads[2].wait()

    def take_flow(k, carry):
        for r in range(0, rows, span):
            east = east_raw[k, pl.ds(r, span), :].astype(jnp.float32)
            north = north_raw[k, pl.ds(r, span), :].astype(jnp.float32)
            east_pad[k, pl.ds(PAD + r, span), :] = east
            north_pad[k, pl.ds(PAD + r, span), :] = north
            put_side(flow_side, r, [(k, east), (kl + k, north)])
        return carry

    lax.fori_loop(0, kl, take_flow, 0)
    rows_out(east_pad, flow_out, 0, kl)
    rows_out(north_pad, flow_out, 2 * kl, kl)
    flow_copies.start()
    for copy in flow_rows:
        copy.start()

    for load in loads[3:]:
        load.wait()
    bunch = 4

    def pack(g, carry):
        for r in range(0, rows, span):
            pieces = []
            for j in range(bunch):
                i = g * bunch + j
                pieces.append((i, q0[i, pl.ds(PAD + r, span), :]))
            put_side(q_side, r, pieces)
        return carry

    lax.fori_loop(0, planes // bunch, pack, 0)
    q_copies.start()
    rows_out(q0, row_out, 0, planes)
    for copy in q_rows:
        copy.start()

    level_copies.wait_recv()
    lane_ext = lanes(ext)
    north_lanes = jnp.where(has_north, cols, 0)
    south_lanes = jnp.where(has_south, cols, 0)

    def known(north, south, lane):
        return (
            jnp.where(lane < north_lanes, north, 0.0),
            jnp.where(lane < south_lanes, south, 0.0),
        )

    def join(parts):
        north, south = known(parts[1], parts[2], lane_ext)
        return jnp.concatenate(
            [parts[0], jnp.where(lane_ext < cols // 2, north, south)], axis=1
        )

    def neighbours(value):
        return (
            pltpu.roll(value, ext - 1, 0), pltpu.roll(value, 1, 0),
            pltpu.roll(value, 2 * cols - 1, 1), pltpu.roll(value, 1, 1),
        )

    trim = PAD - HALO
    depth = join(
        [level_ext[n].astype(jnp.float32)[trim : trim + ext] for n in range(3)]
    ) / kl
    sides = [jnp.minimum(depth, other) for other in neighbours(depth)]
    diagonal = ALPHA * depth + (depth == 0.0).astype(jnp.float32)
    diagonal = diagonal + sides[0] + sides[1] + sides[2] + sides[3]
    inverse = 1.0 / diagonal
    lane = lanes(rows)
    corner = lane & 3
    for n, side in enumerate(sides + [depth]):
        if n < 4:
            operator_ext[n] = -side * inverse
        scaled_side = side * kl
        reach[n] = scaled_side[:, :cols]
        edge = scaled_side[HALO:top, cols:]
        side_reach[n] = jnp.where(corner == 1, edge[:, cols - 1 : cols], edge[:, :1])
    operator_ext[4] = diagonal
    operator_ext[5] = inverse

    def merge(side):
        north, south = known(side[1], side[2], lane_ext)
        return jnp.where((lane_ext & 3) >= 2, north, south)

    def coefficients(level, limit, east, west, north, south):
        def gate(n, value):
            return jnp.where(level < limit(n), value, 0.0)

        def out_of(face):
            return jnp.maximum(face, 0.0) + KAPPA

        def back(face):
            return KAPPA - jnp.minimum(face, 0.0)

        lost = gate(0, out_of(east)) + gate(1, back(west)) + gate(2, out_of(north)) + gate(3, back(south))
        return (
            gate(4, 1.0 - lost), gate(0, back(east)), gate(1, out_of(west)),
            gate(2, back(north)), gate(3, out_of(south)),
        )

    flow_copies.wait_recv()
    for copy in flow_rows:
        copy.wait_recv()
    rows_in(flow_in, east_pad, 0, kl)
    rows_in(flow_in, north_pad, 2 * kl, kl)
    flow_join[...] = merge(flow_side)
    wide = 48
    lane_wide = lanes(wide)

    def prepare(k, carry):
        level = k.astype(jnp.float32)
        for e in range(0, ext, wide):
            part = pl.ds(e, wide)
            east = east_pad[k, pl.ds(HALO + e, wide), :]
            west = east_pad[k, pl.ds(HALO + e - 1, wide), :]
            north = north_pad[k, pl.ds(HALO + e, wide), :]
            halo = pltpu.roll(flow_join[part, :], cols // 2 - 1 - 4 * k, 1)
            south = jnp.where(lane_wide == 0, halo, pltpu.roll(north, 1, 1))
            result = coefficients(level, lambda n: reach[n, part, :], east, west, north, south)
            for ref, value in zip((coef_c, coef_e, coef_w, coef_n, coef_s), result):
                ref[k, part, :] = value
        return carry

    lax.fori_loop(0, kl, prepare, 0)

    half = cols // 2
    joined = flow_join[...]
    turned = pltpu.roll(joined, half, 1)
    east_join[...] = jnp.where(lane_ext < half, joined, turned)
    north_side = jnp.where(lane_ext < half, turned, joined)[HALO:top]
    own_flow = flow_side[0, own, :]
    own_north = jnp.where(lane < half, pltpu.roll(own_flow, half, 1), own_flow)
    south_side = jnp.where(corner == 2, pltpu.roll(own_north, 1, 1), pltpu.roll(north_side, 1, 1))
    side_level = ((lane & (half - 1)) >> 2).astype(jnp.float32)
    side_coef = coefficients(
        side_level, lambda n: side_reach[n],
        east_join[own, :], east_join[pl.ds(HALO - 1, rows), :], north_side, south_side,
    )
    q_copies.wait_recv()
    q_join[...] = merge(q_side)
    here = q_join[own, :]
    own_side = q_side[0, own, :]
    north = jnp.where(corner == 1, pltpu.roll(own_side, cols - 1, 1), pltpu.roll(here, cols - 1, 1))
    south = jnp.where(corner == 2, pltpu.roll(own_side, 1, 1), pltpu.roll(here, 1, 1))
    moved = (
        side_coef[0] * here
        + side_coef[1] * q_join[pl.ds(HALO + 1, rows), :]
        + side_coef[2] * q_join[pl.ds(HALO - 1, rows), :]
        + side_coef[3] * north
        + side_coef[4] * south
    )

    def swap(value, place):
        return jnp.where((place & 3) == 1, pltpu.roll(value, cols - 1, 1), pltpu.roll(value, 1, 1))

    q_swap[0] = swap(q_join[...], lane_ext)
    q_swap[1, own, :] = swap(moved, lane)

    for copy in q_rows:
        copy.wait_recv()
    rows_in(row_in, q0, 0, planes)

    def advance(q, which, i, k, e, count, lane_here):
        part = pl.ds(e, count)
        here = q[i, pl.ds(HALO + e, count), :]
        halo = pltpu.roll(q_swap[which, part, :], cols - 2 - 4 * i, 1)
        north = jnp.where(lane_here == cols - 1, halo, pltpu.roll(here, cols - 1, 1))
        south = jnp.where(lane_here == 0, halo, pltpu.roll(here, 1, 1))
        return (
            coef_c[k, part, :] * here
            + coef_e[k, part, :] * q[i, pl.ds(HALO + e + 1, count), :]
            + coef_w[k, part, :] * q[i, pl.ds(HALO + e - 1, count), :]
            + coef_n[k, part, :] * north
            + coef_s[k, part, :] * south
        )

    def first_step(k, carry):
        for e in range(0, ext, wide):
            for tracer in range(2):
                i = tracer * kl + k
                q1[i, pl.ds(HALO + e, wide), :] = advance(q0, 0, i, k, e, wide, lane_wide)
        return carry

    lax.fori_loop(0, kl, first_step, 0)
    forcing_ext[0, own, :] = jnp.zeros((rows, cols), jnp.float32)
    lane_span = lanes(span)

    def second_step(k, carry):
        for r in range(0, rows, span):
            heat = advance(q1, 1, k, k, HALO + r, span, lane_span)
            salt = advance(q1, 1, kl + k, k, HALO + r, span, lane_span)
            q2[k, pl.ds(r, span), :] = heat
            q2[kl + k, pl.ds(r, span), :] = salt
            forcing_ext[0, pl.ds(HALO + r, span), :] += 0.25 * (heat - 0.8 * salt)
        return carry

    lax.fori_loop(0, kl, second_step, 0)
    forcing_copies.start()

    forcing_copies.wait_recv()
    basis = [join([forcing_ext[0], forcing_ext[1], forcing_ext[2]]) * operator_ext[5]]
    for step in range(ITERS):
        around = neighbours(basis[-1])
        basis.append(sum(operator_ext[n] * around[n] for n in range(4)))
    basis = [vector[HALO:top, :cols] for vector in basis]
    own_diagonal = operator_ext[4, pl.ds(HALO, rows), pl.ds(0, cols)]
    scaled = [own_diagonal * vector for vector in basis[:ITERS]]
    gram_tile[...] = jnp.zeros_like(gram_tile)
    for n in range(2 * ITERS):
        product = scaled[n // 2] * basis[(n + 1) // 2]
        gram_tile[pl.ds(n, 1), :] = jnp.sum(product, axis=0, keepdims=True)

    mine = (lanes(8) >> 4) == lax.broadcasted_iota(jnp.int32, (8, cols), 0)
    tile = gram_tile[...]
    for fold in (cols // 2, cols // 4, cols // 8):
        tile = tile + pltpu.roll(tile, fold, 1)
    gram[0] = jnp.sum(jnp.where(mine, tile, 0.0), axis=0, keepdims=True)
    sum_copies = [
        pltpu.make_async_remote_copy(
            src_ref=gram.at[0],
            dst_ref=gram.at[dx * gy + dy],
            send_sem=sum_send.at[dx * gy + dy],
            recv_sem=sum_recv.at[dx * gy + dy],
            device_id=device(dx, dy),
            device_id_type=MESH,
        )
        for dx, dy in others
    ]
    for copy in sum_copies:
        copy.start()
    for copy in sum_copies:
        copy.wait_recv()
    row = gram[0]
    for n in range(1, gx * gy):
        row = row + gram[n]
    total = jnp.sum(jnp.where(mine, row, 0.0), axis=1, keepdims=True)
    moment = [total[n : n + 1, :] for n in range(2 * ITERS)]

    def inner(left, right):
        terms = [
            a * b * moment[i + j]
            for i, a in enumerate(left) for j, b in enumerate(right)
        ]
        return functools.reduce(lambda x, y: x + y, terms)

    def applied(poly):
        grown = poly + [jnp.zeros_like(poly[0])]
        return [grown[0]] + [grown[n] + grown[n - 1] for n in range(1, len(grown))]

    one = jnp.ones_like(moment[0])
    precond, direction, answer = [one], [one], []
    rz_now = inner(precond, precond)
    for step in range(ITERS):
        image = applied(direction)
        alpha = rz_now / inner(direction, image)
        answer = [
            (answer[n] if n < len(answer) else 0.0) + alpha * direction[n]
            for n in range(len(direction))
        ]
        if step + 1 < ITERS:
            precond = [
                (precond[n] if n < len(precond) else 0.0) - alpha * image[n]
                for n in range(len(image))
            ]
            rz_next = inner(precond, precond)
            beta = rz_next / rz_now
            direction = [
                precond[n] + (beta * direction[n] if n < len(direction) else 0.0)
                for n in range(len(precond))
            ]
            rz_now = rz_next
    pressure[...] = answer[0] * basis[0] + answer[1] * basis[1] + answer[2] * basis[2]

    for exchange in (level_copies, flow_copies, q_copies, forcing_copies):
        exchange.wait_send()
    for copy in flow_rows + q_rows + sum_copies:
        copy.wait_send()


def on_device(gx, gy, tracers, east_flow, north_flow, levels):
    pair, kl, rows, cols = tracers.shape
    planes = pair * kl
    ext = rows + 2 * HALO
    pad = rows + 2 * PAD
    f32 = jnp.float32
    in_hbm = pl.BlockSpec(memory_space=pltpu.HBM)
    plane = (kl, rows, cols)
    wide_plane = (kl, ext, cols)
    new_tracers, pressure = pl.pallas_call(
        functools.partial(fused, gx, gy),
        out_shape=(
            pltpu.VMEM((planes, rows, cols), f32),
            pltpu.VMEM((rows, cols), f32),
        ),
        in_specs=[in_hbm] * 4,
        out_specs=(pl.BlockSpec(memory_space=pltpu.VMEM),) * 2,
        scratch_shapes=[
            pltpu.VMEM((planes, pad, cols), f32),
            pltpu.VMEM((planes, pad, cols), f32),
            pltpu.VMEM(plane, jnp.bfloat16),
            pltpu.VMEM(plane, jnp.bfloat16),
            pltpu.VMEM((kl, pad, cols), f32),
            pltpu.VMEM((kl, pad, cols), f32),
            pltpu.VMEM((rows, cols), jnp.int32),
            pltpu.VMEM((3, pad, cols), jnp.bfloat16),
            pltpu.VMEM(wide_plane, f32),
            pltpu.VMEM(wide_plane, f32),
            pltpu.VMEM(wide_plane, f32),
            pltpu.VMEM(wide_plane, f32),
            pltpu.VMEM(wide_plane, f32),
            pltpu.VMEM((5, ext, cols), f32),
            pltpu.VMEM((5, rows, cols), f32),
            pltpu.VMEM((6, ext, 2 * cols), f32),
            pltpu.VMEM((2, 4 * kl, cols), f32),
            pltpu.VMEM((2, 4 * kl, cols), f32),
            pltpu.VMEM((2, 2 * planes, cols), f32),
            pltpu.VMEM((2, 2 * planes, cols), f32),
            pltpu.VMEM((3, ext, cols), f32),
            pltpu.VMEM((3, ext, cols), f32),
            pltpu.VMEM((ext, cols), f32),
            pltpu.VMEM((ext, cols), f32),
            pltpu.VMEM((ext, cols), f32),
            pltpu.VMEM((2, ext, cols), f32),
            pltpu.VMEM((3, ext, cols), f32),
            pltpu.VMEM((8, cols), f32),
            pltpu.VMEM((gx * gy, 1, cols), f32),
            pltpu.SemaphoreType.DMA((3 + PIECES,)),
            pltpu.SemaphoreType.DMA((4, 8)),
            pltpu.SemaphoreType.DMA((4, 8)),
            pltpu.SemaphoreType.DMA((2, 2)),
            pltpu.SemaphoreType.DMA((2, 2)),
            pltpu.SemaphoreType.DMA((gx * gy,)),
            pltpu.SemaphoreType.DMA((gx * gy,)),
        ],
        compiler_params=pltpu.CompilerParams(
            collective_id=0, has_side_effects=True, vmem_limit_bytes=60 * 1024 * 1024
        ),
    )(tracers.reshape(planes, rows, cols), east_flow, north_flow, levels)
    return new_tracers.reshape(tracers.shape), pressure


def solution(mesh):
    placed = (P(None, None, "gx", "gy"), P(None, "gx", "gy"), P(None, "gx", "gy"), P("gx", "gy"))
    return jax.shard_map(
        functools.partial(on_device, mesh.shape["gx"], mesh.shape["gy"]),
        mesh=mesh,
        in_specs=placed,
        out_specs=(P(None, None, "gx", "gy"), P("gx", "gy")),
        check_vma=False,
    )
```

```python
import functools

import jax
import jax.numpy as jnp
from jax import lax
from jax.experimental import pallas as pl
from jax.experimental.pallas import tpu as pltpu
from jax.sharding import PartitionSpec as P

MESH = pl.DeviceIdType.MESH
ITERS = 3
KAPPA = 0.08
ALPHA = 0.05
HALO = 8
PAD = 16
PIECES = 4


def fused(
    gx, gy,
    tracers, east_flow, north_flow, levels,
    q2, pressure,
    q0, q1_a, q1_b, east_raw, north_raw, east_pad, north_pad, level_block, level_ext,
    coef_a, coef_b, reach, side_reach, operator_ext,
    flow_out, flow_in, row_out, row_in, flow_side, q_side, flow_join, east_join, q_join, q_swap,
    forcing_ext, gram_tile, gram,
    load_sem, ext_send, ext_recv, row_send, row_recv,
    sum_send, sum_recv,
):
    planes, rows, cols = tracers.shape
    kl = planes // 2
    top = HALO + rows
    ext = rows + 2 * HALO
    mx = lax.axis_index("gx")
    my = lax.axis_index("gy")
    own = pl.ds(HALO, rows)

    def device(dx, dy):
        return {"gx": lax.rem(mx + dx + gx, gx), "gy": lax.rem(my + dy + gy, gy)}

    loads = [
        pltpu.make_async_copy(levels, level_block, load_sem.at[0]),
        pltpu.make_async_copy(east_flow, east_raw, load_sem.at[1]),
        pltpu.make_async_copy(north_flow, north_raw, load_sem.at[2]),
    ]
    share = planes // PIECES
    for piece in range(PIECES):
        loads.append(
            pltpu.make_async_copy(
                tracers.at[pl.ds(piece * share, share)],
                q0.at[pl.ds(piece * share, share), pl.ds(PAD, rows)],
                load_sem.at[3 + piece],
            )
        )
    for load in loads:
        load.start()

    others = [(dx, dy) for dx in range(gx) for dy in range(gy) if (dx, dy) != (0, 0)]
    barrier = pltpu.get_barrier_semaphore()
    for dx, dy in others:
        pl.semaphore_signal(barrier, inc=1, device_id=device(dx, dy), device_id_type=MESH)

    has_north = my < gy - 1
    has_south = my > 0

    class Exchange:
        def __init__(self, buffer, which, rim, zonal=True):
            last, first, whole = pl.ds(rows, rim), pl.ds(rim, rim), pl.ds(rim, rows)
            low, high = pl.ds(0, rim), pl.ds(rim + rows, rim)
            plan = [
                (0, 1, whole, 2, whole), (0, -1, whole, 1, whole),
                (1, 1, last, 2, low), (-1, 1, first, 2, high),
                (1, -1, last, 1, low), (-1, -1, first, 1, high),
            ]
            if zonal:
                plan += [(1, 0, last, 0, low), (-1, 0, first, 0, high)]
            self.copies = [
                (
                    dy,
                    pltpu.make_async_remote_copy(
                        src_ref=buffer.at[0, source],
                        dst_ref=buffer.at[slot, place],
                        send_sem=ext_send.at[which, n],
                        recv_sem=ext_recv.at[which, n],
                        device_id=device(dx, dy),
                        device_id_type=MESH,
                    ),
                )
                for n, (dx, dy, source, slot, place) in enumerate(plan)
            ]

        def each(self, outward, action):
            for dy, copy in self.copies:
                if dy == 0:
                    action(copy)
                else:
                    pl.when(has_north if (dy > 0) == outward else has_south)(
                        functools.partial(action, copy)
                    )

        def start(self):
            self.each(True, lambda copy: copy.start())

        def wait_recv(self):
            self.each(False, lambda copy: copy.wait_recv())

        def wait_send(self):
            self.each(True, lambda copy: copy.wait_send())

    def row_copies(source, place, which):
        return [
            pltpu.make_async_remote_copy(
                src_ref=source.at[n],
                dst_ref=place.at[n],
                send_sem=row_send.at[which, n],
                recv_sem=row_recv.at[which, n],
                device_id=device(1 - 2 * n, 0),
                device_id_type=MESH,
            )
            for n in range(2)
        ]

    def lanes(count):
        return lax.broadcasted_iota(jnp.int32, (count, cols), 1)

    def rows_out(source, target, base, count):
        for i in range(count):
            target[0, pl.ds(base + 2 * i, 2), :] = source[i, pl.ds(PAD + rows - 2, 2), :]
            target[1, pl.ds(base + 2 * i, 2), :] = source[i, pl.ds(PAD, 2), :]

    def rows_in(source, target, base, count):
        for i in range(count):
            target[i, pl.ds(PAD - 2, 2), :] = source[0, pl.ds(base + 2 * i, 2), :]
            target[i, pl.ds(PAD + rows, 2), :] = source[1, pl.ds(base + 2 * i, 2), :]

    span = 32
    group = lanes(span) >> 2

    def put_side(target, r, pieces):
        place = pl.ds(HALO + r, span)
        total = target[0, place, :]
        for index, value in pieces:
            total = jnp.where(group == index, pltpu.roll(value, 4 * index + 2, 1), total)
        target[0, place, :] = total

    level_copies = Exchange(level_ext, 0, PAD)
    flow_copies = Exchange(flow_side, 1, HALO, zonal=False)
    q_copies = Exchange(q_side, 2, HALO, zonal=False)
    forcing_copies = Exchange(forcing_ext, 3, HALO)
    flow_rows = row_copies(flow_out, flow_in, 0)
    q_rows = row_copies(row_out, row_in, 1)
    flow_side[0] = jnp.zeros_like(flow_side[0])
    q_side[0] = jnp.zeros_like(q_side[0])
    loads[0].wait()
    level_ext[0, pl.ds(PAD, rows), :] = level_block[...].astype(jnp.float32).astype(jnp.bfloat16)
    pl.semaphore_wait(barrier, len(others))
    level_copies.start()
    loads[1].wait()
    loads[2].wait()

    def take_flow(k, carry):
        for r in range(0, rows, span):
            east = east_raw[k, pl.ds(r, span), :].astype(jnp.float32)
            north = north_raw[k, pl.ds(r, span), :].astype(jnp.float32)
            east_pad[k, pl.ds(PAD + r, span), :] = east
            north_pad[k, pl.ds(PAD + r, span), :] = north
            put_side(flow_side, r, [(k, east), (kl + k, north)])
        return carry

    lax.fori_loop(0, kl, take_flow, 0)
    rows_out(east_pad, flow_out, 0, kl)
    rows_out(north_pad, flow_out, 2 * kl, kl)
    flow_copies.start()
    for copy in flow_rows:
        copy.start()

    for load in loads[3:]:
        load.wait()
    bunch = 4

    def pack(g, carry):
        for r in range(0, rows, span):
            pieces = []
            for j in range(bunch):
                i = g * bunch + j
                pieces.append((i, q0[i, pl.ds(PAD + r, span), :]))
            put_side(q_side, r, pieces)
        return carry

    lax.fori_loop(0, planes // bunch, pack, 0)
    q_copies.start()
    rows_out(q0, row_out, 0, planes)
    for copy in q_rows:
        copy.start()

    level_copies.wait_recv()
    lane_ext = lanes(ext)
    north_lanes = jnp.where(has_north, cols, 0)
    south_lanes = jnp.where(has_south, cols, 0)

    def known(north, south, lane):
        return (
            jnp.where(lane < north_lanes, north, 0.0),
            jnp.where(lane < south_lanes, south, 0.0),
        )

    def join(parts):
        north, south = known(parts[1], parts[2], lane_ext)
        return jnp.concatenate(
            [parts[0], jnp.where(lane_ext < cols // 2, north, south)], axis=1
        )

    def neighbours(value):
        return (
            pltpu.roll(value, ext - 1, 0), pltpu.roll(value, 1, 0),
            pltpu.roll(value, 2 * cols - 1, 1), pltpu.roll(value, 1, 1),
        )

    trim = PAD - HALO
    depth = join(
        [level_ext[n].astype(jnp.float32)[trim : trim + ext] for n in range(3)]
    ) / kl
    sides = [jnp.minimum(depth, other) for other in neighbours(depth)]
    diagonal = ALPHA * depth + (depth == 0.0).astype(jnp.float32)
    diagonal = diagonal + sides[0] + sides[1] + sides[2] + sides[3]
    inverse = 1.0 / diagonal
    lane = lanes(rows)
    corner = lane & 3
    for n, side in enumerate(sides + [depth]):
        if n < 4:
            operator_ext[n] = -side * inverse
        scaled_side = side * kl
        reach[n] = scaled_side[:, :cols]
        edge = scaled_side[HALO:top, cols:]
        side_reach[n] = jnp.where(corner == 1, edge[:, cols - 1 : cols], edge[:, :1])
    operator_ext[4] = diagonal
    operator_ext[5] = inverse

    def merge(side):
        north, south = known(side[1], side[2], lane_ext)
        return jnp.where((lane_ext & 3) >= 2, north, south)

    def coefficients(level, limit, east, west, north, south):
        def gate(n, value):
            return jnp.where(level < limit(n), value, 0.0)

        def out_of(face):
            return jnp.maximum(face, 0.0) + KAPPA

        def back(face):
            return KAPPA - jnp.minimum(face, 0.0)

        lost = gate(0, out_of(east)) + gate(1, back(west)) + gate(2, out_of(north)) + gate(3, back(south))
        return (
            gate(4, 1.0 - lost), gate(0, back(east)), gate(1, out_of(west)),
            gate(2, back(north)), gate(3, out_of(south)),
        )

    flow_copies.wait_recv()
    for copy in flow_rows:
        copy.wait_recv()
    rows_in(flow_in, east_pad, 0, kl)
    rows_in(flow_in, north_pad, 2 * kl, kl)
    flow_join[...] = merge(flow_side)
    half = cols // 2
    joined = flow_join[...]
    turned = pltpu.roll(joined, half, 1)
    east_join[...] = jnp.where(lane_ext < half, joined, turned)
    north_side = jnp.where(lane_ext < half, turned, joined)[HALO:top]
    own_flow = flow_side[0, own, :]
    own_north = jnp.where(lane < half, pltpu.roll(own_flow, half, 1), own_flow)
    south_side = jnp.where(corner == 2, pltpu.roll(own_north, 1, 1), pltpu.roll(north_side, 1, 1))
    side_level = ((lane & (half - 1)) >> 2).astype(jnp.float32)
    side_coef = coefficients(
        side_level, lambda n: side_reach[n],
        east_join[own, :], east_join[pl.ds(HALO - 1, rows), :], north_side, south_side,
    )
    q_copies.wait_recv()
    q_join[...] = merge(q_side)
    here = q_join[own, :]
    own_side = q_side[0, own, :]
    north = jnp.where(corner == 1, pltpu.roll(own_side, cols - 1, 1), pltpu.roll(here, cols - 1, 1))
    south = jnp.where(corner == 2, pltpu.roll(own_side, 1, 1), pltpu.roll(here, 1, 1))
    moved = (
        side_coef[0] * here
        + side_coef[1] * q_join[pl.ds(HALO + 1, rows), :]
        + side_coef[2] * q_join[pl.ds(HALO - 1, rows), :]
        + side_coef[3] * north
        + side_coef[4] * south
    )

    def swap(value, place):
        return jnp.where((place & 3) == 1, pltpu.roll(value, cols - 1, 1), pltpu.roll(value, 1, 1))

    q_swap[0] = swap(q_join[...], lane_ext)
    q_swap[1, own, :] = swap(moved, lane)

    for copy in q_rows:
        copy.wait_recv()
    rows_in(row_in, q0, 0, planes)

    wide = 24
    lane_wide = lanes(wide)
    lane_span = lanes(span)
    forcing_ext[0, own, :] = jnp.zeros((rows, cols), jnp.float32)

    def advance(here, east, west, halo, coef, lane_here):
        north = jnp.where(lane_here == cols - 1, halo, pltpu.roll(here, cols - 1, 1))
        south = jnp.where(lane_here == 0, halo, pltpu.roll(here, 1, 1))
        return (
            coef[0] * here + coef[1] * east + coef[2] * west
            + coef[3] * north + coef[4] * south
        )

    def first_step(k, coef_ref, q_ref, e):
        part = pl.ds(e, wide)
        level = lax.convert_element_type(k, jnp.float32)
        east = east_pad[k, pl.ds(HALO + e, wide), :]
        west = east_pad[k, pl.ds(HALO + e - 1, wide), :]
        north = north_pad[k, pl.ds(HALO + e, wide), :]
        halo = pltpu.roll(flow_join[part, :], cols // 2 - 1 - 4 * k, 1)
        south = jnp.where(lane_wide == 0, halo, pltpu.roll(north, 1, 1))
        coef = coefficients(level, lambda n: reach[n, part, :], east, west, north, south)
        for n in range(5):
            coef_ref[n, part, :] = coef[n]
        for tracer in range(2):
            i = tracer * kl + k
            q_ref[tracer, pl.ds(HALO + e, wide), :] = advance(
                q0[i, pl.ds(HALO + e, wide), :],
                q0[i, pl.ds(HALO + e + 1, wide), :],
                q0[i, pl.ds(HALO + e - 1, wide), :],
                pltpu.roll(q_swap[0, part, :], cols - 2 - 4 * i, 1),
                coef, lane_wide,
            )

    def second_step(k, coef_ref, q_ref, r):
        part = pl.ds(HALO + r, span)
        coef = [coef_ref[n, part, :] for n in range(5)]
        result = []
        for tracer in range(2):
            i = tracer * kl + k
            value = advance(
                q_ref[tracer, pl.ds(PAD + r, span), :],
                q_ref[tracer, pl.ds(PAD + r + 1, span), :],
                q_ref[tracer, pl.ds(PAD + r - 1, span), :],
                pltpu.roll(q_swap[1, part, :], cols - 2 - 4 * i, 1),
                coef, lane_span,
            )
            q2[i, pl.ds(r, span), :] = value
            result.append(value)
        forcing_ext[0, part, :] += 0.25 * (result[0] - 0.8 * result[1])

    def beside(first, second):
        ahead = [functools.partial(first_step, *first, e) for e in range(0, ext, wide)] if first else []
        behind = [functools.partial(second_step, *second, r) for r in range(0, rows, span)] if second else []
        for n in range(max(len(ahead), len(behind))):
            for chunks in (ahead, behind):
                if n < len(chunks):
                    chunks[n]()

    slot_a, slot_b = (coef_a, q1_a), (coef_b, q1_b)
    beside((0, *slot_a), None)

    def two_levels(j, carry):
        k = 2 * j
        beside((k + 1, *slot_b), (k, *slot_a))
        beside((k + 2, *slot_a), (k + 1, *slot_b))
        return carry

    lax.fori_loop(0, kl // 2 - 1, two_levels, 0)
    beside((kl - 1, *slot_b), (kl - 2, *slot_a))
    beside(None, (kl - 1, *slot_b))
    forcing_copies.start()

    forcing_copies.wait_recv()
    basis = [join([forcing_ext[0], forcing_ext[1], forcing_ext[2]]) * operator_ext[5]]
    for step in range(ITERS):
        around = neighbours(basis[-1])
        basis.append(sum(operator_ext[n] * around[n] for n in range(4)))
    basis = [vector[HALO:top, :cols] for vector in basis]
    own_diagonal = operator_ext[4, pl.ds(HALO, rows), pl.ds(0, cols)]
    scaled = [own_diagonal * vector for vector in basis[:ITERS]]
    gram_tile[...] = jnp.zeros_like(gram_tile)
    for n in range(2 * ITERS):
        product = scaled[n // 2] * basis[(n + 1) // 2]
        gram_tile[pl.ds(n, 1), :] = jnp.sum(product, axis=0, keepdims=True)

    mine = (lanes(8) >> 4) == lax.broadcasted_iota(jnp.int32, (8, cols), 0)
    tile = gram_tile[...]
    for fold in (cols // 2, cols // 4, cols // 8):
        tile = tile + pltpu.roll(tile, fold, 1)
    gram[0] = jnp.sum(jnp.where(mine, tile, 0.0), axis=0, keepdims=True)
    sum_copies = [
        pltpu.make_async_remote_copy(
            src_ref=gram.at[0],
            dst_ref=gram.at[dx * gy + dy],
            send_sem=sum_send.at[dx * gy + dy],
            recv_sem=sum_recv.at[dx * gy + dy],
            device_id=device(dx, dy),
            device_id_type=MESH,
        )
        for dx, dy in others
    ]
    for copy in sum_copies:
        copy.start()
    for copy in sum_copies:
        copy.wait_recv()
    row = gram[0]
    for n in range(1, gx * gy):
        row = row + gram[n]
    total = jnp.sum(jnp.where(mine, row, 0.0), axis=1, keepdims=True)
    moment = [total[n : n + 1, :] for n in range(2 * ITERS)]

    def inner(left, right):
        terms = [
            a * b * moment[i + j]
            for i, a in enumerate(left) for j, b in enumerate(right)
        ]
        return functools.reduce(lambda x, y: x + y, terms)

    def applied(poly):
        grown = poly + [jnp.zeros_like(poly[0])]
        return [grown[0]] + [grown[n] + grown[n - 1] for n in range(1, len(grown))]

    one = jnp.ones_like(moment[0])
    precond, direction, answer = [one], [one], []
    rz_now = inner(precond, precond)
    for step in range(ITERS):
        image = applied(direction)
        alpha = rz_now / inner(direction, image)
        answer = [
            (answer[n] if n < len(answer) else 0.0) + alpha * direction[n]
            for n in range(len(direction))
        ]
        if step + 1 < ITERS:
            precond = [
                (precond[n] if n < len(precond) else 0.0) - alpha * image[n]
                for n in range(len(image))
            ]
            rz_next = inner(precond, precond)
            beta = rz_next / rz_now
            direction = [
                precond[n] + (beta * direction[n] if n < len(direction) else 0.0)
                for n in range(len(precond))
            ]
            rz_now = rz_next
    pressure[...] = answer[0] * basis[0] + answer[1] * basis[1] + answer[2] * basis[2]

    for exchange in (level_copies, flow_copies, q_copies, forcing_copies):
        exchange.wait_send()
    for copy in flow_rows + q_rows + sum_copies:
        copy.wait_send()


def on_device(gx, gy, tracers, east_flow, north_flow, levels):
    pair, kl, rows, cols = tracers.shape
    planes = pair * kl
    ext = rows + 2 * HALO
    pad = rows + 2 * PAD
    f32 = jnp.float32
    in_hbm = pl.BlockSpec(memory_space=pltpu.HBM)
    plane = (kl, rows, cols)
    new_tracers, pressure = pl.pallas_call(
        functools.partial(fused, gx, gy),
        out_shape=(
            pltpu.VMEM((planes, rows, cols), f32),
            pltpu.VMEM((rows, cols), f32),
        ),
        in_specs=[in_hbm] * 4,
        out_specs=(pl.BlockSpec(memory_space=pltpu.VMEM),) * 2,
        scratch_shapes=[
            pltpu.VMEM((planes, pad, cols), f32),
            pltpu.VMEM((2, pad, cols), f32),
            pltpu.VMEM((2, pad, cols), f32),
            pltpu.VMEM(plane, jnp.bfloat16),
            pltpu.VMEM(plane, jnp.bfloat16),
            pltpu.VMEM((kl, pad, cols), f32),
            pltpu.VMEM((kl, pad, cols), f32),
            pltpu.VMEM((rows, cols), jnp.int32),
            pltpu.VMEM((3, pad, cols), jnp.bfloat16),
            pltpu.VMEM((5, ext, cols), f32),
            pltpu.VMEM((5, ext, cols), f32),
            pltpu.VMEM((5, ext, cols), f32),
            pltpu.VMEM((5, rows, cols), f32),
            pltpu.VMEM((6, ext, 2 * cols), f32),
            pltpu.VMEM((2, 4 * kl, cols), f32),
            pltpu.VMEM((2, 4 * kl, cols), f32),
            pltpu.VMEM((2, 2 * planes, cols), f32),
            pltpu.VMEM((2, 2 * planes, cols), f32),
            pltpu.VMEM((3, ext, cols), f32),
            pltpu.VMEM((3, ext, cols), f32),
            pltpu.VMEM((ext, cols), f32),
            pltpu.VMEM((ext, cols), f32),
            pltpu.VMEM((ext, cols), f32),
            pltpu.VMEM((2, ext, cols), f32),
            pltpu.VMEM((3, ext, cols), f32),
            pltpu.VMEM((8, cols), f32),
            pltpu.VMEM((gx * gy, 1, cols), f32),
            pltpu.SemaphoreType.DMA((3 + PIECES,)),
            pltpu.SemaphoreType.DMA((4, 8)),
            pltpu.SemaphoreType.DMA((4, 8)),
            pltpu.SemaphoreType.DMA((2, 2)),
            pltpu.SemaphoreType.DMA((2, 2)),
            pltpu.SemaphoreType.DMA((gx * gy,)),
            pltpu.SemaphoreType.DMA((gx * gy,)),
        ],
        compiler_params=pltpu.CompilerParams(
            collective_id=0, has_side_effects=True, vmem_limit_bytes=60 * 1024 * 1024
        ),
    )(tracers.reshape(planes, rows, cols), east_flow, north_flow, levels)
    return new_tracers.reshape(tracers.shape), pressure


def solution(mesh):
    placed = (P(None, None, "gx", "gy"), P(None, "gx", "gy"), P(None, "gx", "gy"), P("gx", "gy"))
    return jax.shard_map(
        functools.partial(on_device, mesh.shape["gx"], mesh.shape["gy"]),
        mesh=mesh,
        in_specs=placed,
        out_specs=(P(None, None, "gx", "gy"), P("gx", "gy")),
        check_vma=False,
    )
```

```python
import functools

import jax
import jax.numpy as jnp
from jax import lax
from jax.experimental import pallas as pl
from jax.experimental.pallas import tpu as pltpu
from jax.sharding import PartitionSpec as P

MESH = pl.DeviceIdType.MESH
ITERS = 3
KAPPA = 0.08
ALPHA = 0.05
HALO = 8
PAD = 16
PIECES = 4


def fused(
    gx, gy,
    tracers, east_flow, north_flow, levels,
    q2, pressure,
    q0, q1_a, q1_b, east_raw, north_raw, east_pad, north_pad, level_block, level_ext,
    coef_a, coef_b, reach, side_reach, operator_ext,
    flow_out, flow_in, row_out, row_in, flow_side, q_side, flow_join, east_join, q_join, q_swap,
    forcing_ext, gram_tile, gram,
    load_sem, ext_send, ext_recv, row_send, row_recv,
    sum_send, sum_recv,
):
    planes, rows, cols = tracers.shape
    kl = planes // 2
    top = HALO + rows
    ext = rows + 2 * HALO
    mx = lax.axis_index("gx")
    my = lax.axis_index("gy")
    own = pl.ds(HALO, rows)

    def device(dx, dy):
        return {"gx": lax.rem(mx + dx + gx, gx), "gy": lax.rem(my + dy + gy, gy)}

    loads = [
        pltpu.make_async_copy(levels, level_block, load_sem.at[0]),
        pltpu.make_async_copy(east_flow, east_raw, load_sem.at[1]),
        pltpu.make_async_copy(north_flow, north_raw, load_sem.at[2]),
    ]
    share = planes // PIECES
    for piece in range(PIECES):
        loads.append(
            pltpu.make_async_copy(
                tracers.at[pl.ds(piece * share, share)],
                q0.at[pl.ds(piece * share, share), pl.ds(PAD, rows)],
                load_sem.at[3 + piece],
            )
        )
    for load in loads:
        load.start()

    others = [(dx, dy) for dx in range(gx) for dy in range(gy) if (dx, dy) != (0, 0)]
    barrier = pltpu.get_barrier_semaphore()
    for dx, dy in others:
        pl.semaphore_signal(barrier, inc=1, device_id=device(dx, dy), device_id_type=MESH)

    has_north = my < gy - 1
    has_south = my > 0

    class Exchange:
        def __init__(self, buffer, which, rim, zonal=True):
            last, first, whole = pl.ds(rows, rim), pl.ds(rim, rim), pl.ds(rim, rows)
            low, high = pl.ds(0, rim), pl.ds(rim + rows, rim)
            plan = [
                (0, 1, whole, 2, whole), (0, -1, whole, 1, whole),
                (1, 1, last, 2, low), (-1, 1, first, 2, high),
                (1, -1, last, 1, low), (-1, -1, first, 1, high),
            ]
            if zonal:
                plan += [(1, 0, last, 0, low), (-1, 0, first, 0, high)]
            self.copies = [
                (
                    dy,
                    pltpu.make_async_remote_copy(
                        src_ref=buffer.at[0, source],
                        dst_ref=buffer.at[slot, place],
                        send_sem=ext_send.at[which, n],
                        recv_sem=ext_recv.at[which, n],
                        device_id=device(dx, dy),
                        device_id_type=MESH,
                    ),
                )
                for n, (dx, dy, source, slot, place) in enumerate(plan)
            ]

        def each(self, outward, action):
            for dy, copy in self.copies:
                if dy == 0:
                    action(copy)
                else:
                    pl.when(has_north if (dy > 0) == outward else has_south)(
                        functools.partial(action, copy)
                    )

        def start(self):
            self.each(True, lambda copy: copy.start())

        def wait_recv(self):
            self.each(False, lambda copy: copy.wait_recv())

        def wait_send(self):
            self.each(True, lambda copy: copy.wait_send())

    def row_copies(source, place, which):
        return [
            pltpu.make_async_remote_copy(
                src_ref=source.at[n],
                dst_ref=place.at[n],
                send_sem=row_send.at[which, n],
                recv_sem=row_recv.at[which, n],
                device_id=device(1 - 2 * n, 0),
                device_id_type=MESH,
            )
            for n in range(2)
        ]

    def lanes(count):
        return lax.broadcasted_iota(jnp.int32, (count, cols), 1)

    def row_of(ref, row):
        count, height, _ = ref.shape
        return ref.reshape(count * height, cols), pl.ds(row, count, stride=height)

    def rows_out(source, target, base, count):
        for n, first in ((0, PAD + rows - 2), (1, PAD)):
            for j in range(2):
                flat, place = row_of(source, first + j)
                target[n, pl.ds(base + j * count, count), :] = flat[place, :]

    def rows_in(source, target, base, count):
        for n, first in ((0, PAD - 2), (1, PAD + rows)):
            for j in range(2):
                flat, place = row_of(target, first + j)
                flat[place, :] = source[n, pl.ds(base + j * count, count), :]

    span = 32
    group = lanes(span) >> 2

    def put_side(target, r, pieces):
        place = pl.ds(HALO + r, span)
        total = target[0, place, :]
        for index, value in pieces:
            total = jnp.where(group == index, pltpu.roll(value, 4 * index + 2, 1), total)
        target[0, place, :] = total

    level_copies = Exchange(level_ext, 0, PAD)
    flow_copies = Exchange(flow_side, 1, HALO, zonal=False)
    q_copies = Exchange(q_side, 2, HALO, zonal=False)
    forcing_copies = Exchange(forcing_ext, 3, HALO)
    flow_rows = row_copies(flow_out, flow_in, 0)
    q_rows = row_copies(row_out, row_in, 1)
    flow_side[0] = jnp.zeros_like(flow_side[0])
    q_side[0] = jnp.zeros_like(q_side[0])
    loads[0].wait()
    level_ext[0, pl.ds(PAD, rows), :] = level_block[...].astype(jnp.float32).astype(jnp.bfloat16)
    pl.semaphore_wait(barrier, len(others))
    level_copies.start()
    loads[1].wait()
    loads[2].wait()

    def take_flow(g, carry):
        for r in range(0, rows, span):
            pieces = []
            for j in range(2):
                k = 2 * g + j
                east = east_raw[k, pl.ds(r, span), :].astype(jnp.float32)
                north = north_raw[k, pl.ds(r, span), :].astype(jnp.float32)
                east_pad[k, pl.ds(PAD + r, span), :] = east
                north_pad[k, pl.ds(PAD + r, span), :] = north
                pieces += [(k, east), (kl + k, north)]
            put_side(flow_side, r, pieces)
        return carry

    lax.fori_loop(0, kl // 2, take_flow, 0)
    rows_out(east_pad, flow_out, 0, kl)
    rows_out(north_pad, flow_out, 2 * kl, kl)
    flow_copies.start()
    for copy in flow_rows:
        copy.start()

    for load in loads[3:]:
        load.wait()
    bunch = 4

    def pack(g, carry):
        for r in range(0, rows, span):
            pieces = []
            for j in range(bunch):
                i = g * bunch + j
                pieces.append((i, q0[i, pl.ds(PAD + r, span), :]))
            put_side(q_side, r, pieces)
        return carry

    lax.fori_loop(0, planes // bunch, pack, 0)
    q_copies.start()
    rows_out(q0, row_out, 0, planes)
    for copy in q_rows:
        copy.start()

    level_copies.wait_recv()
    lane_ext = lanes(ext)
    north_lanes = jnp.where(has_north, cols, 0)
    south_lanes = jnp.where(has_south, cols, 0)

    def known(north, south, lane):
        return (
            jnp.where(lane < north_lanes, north, 0.0),
            jnp.where(lane < south_lanes, south, 0.0),
        )

    def join(parts):
        north, south = known(parts[1], parts[2], lane_ext)
        return jnp.concatenate(
            [parts[0], jnp.where(lane_ext < cols // 2, north, south)], axis=1
        )

    def neighbours(value):
        return (
            pltpu.roll(value, ext - 1, 0), pltpu.roll(value, 1, 0),
            pltpu.roll(value, 2 * cols - 1, 1), pltpu.roll(value, 1, 1),
        )

    trim = PAD - HALO
    depth = join(
        [level_ext[n].astype(jnp.float32)[trim : trim + ext] for n in range(3)]
    ) / kl
    sides = [jnp.minimum(depth, other) for other in neighbours(depth)]
    diagonal = ALPHA * depth + (depth == 0.0).astype(jnp.float32)
    diagonal = diagonal + sides[0] + sides[1] + sides[2] + sides[3]
    inverse = 1.0 / diagonal
    lane = lanes(rows)
    corner = lane & 3
    for n, side in enumerate(sides + [depth]):
        if n < 4:
            operator_ext[n] = -side * inverse
        scaled_side = side * kl
        reach[n] = scaled_side[:, :cols]
        edge = scaled_side[HALO:top, cols:]
        side_reach[n] = jnp.where(corner == 1, edge[:, cols - 1 : cols], edge[:, :1])
    operator_ext[4] = diagonal
    operator_ext[5] = inverse

    def merge(side):
        north, south = known(side[1], side[2], lane_ext)
        return jnp.where((lane_ext & 3) >= 2, north, south)

    def coefficients(level, limit, east, west, north, south):
        def gate(n, value):
            return jnp.where(level < limit(n), value, 0.0)

        def out_of(face):
            return jnp.maximum(face, 0.0) + KAPPA

        def back(face):
            return KAPPA - jnp.minimum(face, 0.0)

        lost = gate(0, out_of(east)) + gate(1, back(west)) + gate(2, out_of(north)) + gate(3, back(south))
        return (
            gate(4, 1.0 - lost), gate(0, back(east)), gate(1, out_of(west)),
            gate(2, back(north)), gate(3, out_of(south)),
        )

    flow_copies.wait_recv()
    for copy in flow_rows:
        copy.wait_recv()
    rows_in(flow_in, east_pad, 0, kl)
    rows_in(flow_in, north_pad, 2 * kl, kl)
    flow_join[...] = merge(flow_side)
    half = cols // 2
    joined = flow_join[...]
    turned = pltpu.roll(joined, half, 1)
    east_join[...] = jnp.where(lane_ext < half, joined, turned)
    north_side = jnp.where(lane_ext < half, turned, joined)[HALO:top]
    own_flow = flow_side[0, own, :]
    own_north = jnp.where(lane < half, pltpu.roll(own_flow, half, 1), own_flow)
    south_side = jnp.where(corner == 2, pltpu.roll(own_north, 1, 1), pltpu.roll(north_side, 1, 1))
    side_level = ((lane & (half - 1)) >> 2).astype(jnp.float32)
    side_coef = coefficients(
        side_level, lambda n: side_reach[n],
        east_join[own, :], east_join[pl.ds(HALO - 1, rows), :], north_side, south_side,
    )
    q_copies.wait_recv()
    q_join[...] = merge(q_side)
    here = q_join[own, :]
    own_side = q_side[0, own, :]
    north = jnp.where(corner == 1, pltpu.roll(own_side, cols - 1, 1), pltpu.roll(here, cols - 1, 1))
    south = jnp.where(corner == 2, pltpu.roll(own_side, 1, 1), pltpu.roll(here, 1, 1))
    moved = (
        side_coef[0] * here
        + side_coef[1] * q_join[pl.ds(HALO + 1, rows), :]
        + side_coef[2] * q_join[pl.ds(HALO - 1, rows), :]
        + side_coef[3] * north
        + side_coef[4] * south
    )

    def swap(value, place):
        return jnp.where((place & 3) == 1, pltpu.roll(value, cols - 1, 1), pltpu.roll(value, 1, 1))

    q_swap[0] = swap(q_join[...], lane_ext)
    q_swap[1, own, :] = swap(moved, lane)

    for copy in q_rows:
        copy.wait_recv()
    rows_in(row_in, q0, 0, planes)

    wide = 24
    lane_wide = lanes(wide)
    lane_span = lanes(span)
    forcing_ext[0, own, :] = jnp.zeros((rows, cols), jnp.float32)

    def advance(here, east, west, halo, coef, lane_here):
        north = jnp.where(lane_here == cols - 1, halo, pltpu.roll(here, cols - 1, 1))
        south = jnp.where(lane_here == 0, halo, pltpu.roll(here, 1, 1))
        return (
            coef[0] * here + coef[1] * east + coef[2] * west
            + coef[3] * north + coef[4] * south
        )

    def first_step(k, coef_ref, q_ref, e):
        part = pl.ds(e, wide)
        level = lax.convert_element_type(k, jnp.float32)
        east = east_pad[k, pl.ds(HALO + e, wide), :]
        north = north_pad[k, pl.ds(HALO + e, wide), :]
        halo = pltpu.roll(flow_join[part, :], cols // 2 - 1 - 4 * k, 1)
        south = jnp.where(lane_wide == 0, halo, pltpu.roll(north, 1, 1))

        def gated(n, face):
            is_open = level < reach[n, part, :]
            face = jnp.where(is_open, face, 0.0)
            out = jnp.maximum(face, 0.0) + jnp.where(is_open, KAPPA, 0.0)
            return out, out - face

        east_out, east_back = gated(0, east)
        coef_ref[1, pl.ds(HALO + e, wide), :] = east_back
        coef_ref[2, pl.ds(HALO + e, wide), :] = east_out
        north_out, north_back = gated(2, north)
        south_out, south_back = gated(3, south)
        west_back = coef_ref[1, pl.ds(HALO + e - 1, wide), :]
        west_out = coef_ref[2, pl.ds(HALO + e - 1, wide), :]
        lost = east_out + west_back + north_out + south_back
        centre = jnp.where(level < reach[4, part, :], 1.0 - lost, 0.0)
        coef = (centre, east_back, west_out, north_back, south_out)
        for n in (0, 3, 4):
            coef_ref[n, pl.ds(HALO + e, wide), :] = coef[n]
        for tracer in range(2):
            i = tracer * kl + k
            q_ref[tracer, pl.ds(HALO + e, wide), :] = advance(
                q0[i, pl.ds(HALO + e, wide), :],
                q0[i, pl.ds(HALO + e + 1, wide), :],
                q0[i, pl.ds(HALO + e - 1, wide), :],
                pltpu.roll(q_swap[0, part, :], cols - 2 - 4 * i, 1),
                coef, lane_wide,
            )

    def second_step(k, coef_ref, q_ref, r):
        part = pl.ds(HALO + r, span)
        coef = [coef_ref[n, pl.ds(PAD + r - (n == 2), span), :] for n in range(5)]
        result = []
        for tracer in range(2):
            i = tracer * kl + k
            value = advance(
                q_ref[tracer, pl.ds(PAD + r, span), :],
                q_ref[tracer, pl.ds(PAD + r + 1, span), :],
                q_ref[tracer, pl.ds(PAD + r - 1, span), :],
                pltpu.roll(q_swap[1, part, :], cols - 2 - 4 * i, 1),
                coef, lane_span,
            )
            q2[i, pl.ds(r, span), :] = value
            result.append(value)
        forcing_ext[0, part, :] += 0.25 * (result[0] - 0.8 * result[1])

    def beside(first, second):
        ahead = [functools.partial(first_step, *first, e) for e in range(0, ext, wide)] if first else []
        behind = [functools.partial(second_step, *second, r) for r in range(0, rows, span)] if second else []
        for n in range(max(len(ahead), len(behind))):
            for chunks in (ahead, behind):
                if n < len(chunks):
                    chunks[n]()

    slot_a, slot_b = (coef_a, q1_a), (coef_b, q1_b)
    beside((0, *slot_a), None)

    def two_levels(j, carry):
        k = 2 * j
        beside((k + 1, *slot_b), (k, *slot_a))
        beside((k + 2, *slot_a), (k + 1, *slot_b))
        return carry

    lax.fori_loop(0, kl // 2 - 1, two_levels, 0)
    beside((kl - 1, *slot_b), (kl - 2, *slot_a))
    beside(None, (kl - 1, *slot_b))
    forcing_copies.start()

    forcing_copies.wait_recv()
    basis = [join([forcing_ext[0], forcing_ext[1], forcing_ext[2]]) * operator_ext[5]]
    for step in range(ITERS):
        around = neighbours(basis[-1])
        basis.append(sum(operator_ext[n] * around[n] for n in range(4)))
    basis = [vector[HALO:top, :cols] for vector in basis]
    own_diagonal = operator_ext[4, pl.ds(HALO, rows), pl.ds(0, cols)]
    scaled = [own_diagonal * vector for vector in basis[:ITERS]]
    gram_tile[...] = jnp.zeros_like(gram_tile)
    for n in range(2 * ITERS):
        product = scaled[n // 2] * basis[(n + 1) // 2]
        gram_tile[pl.ds(n, 1), :] = jnp.sum(product, axis=0, keepdims=True)

    mine = (lanes(8) >> 4) == lax.broadcasted_iota(jnp.int32, (8, cols), 0)
    tile = gram_tile[...]
    for fold in (cols // 2, cols // 4, cols // 8):
        tile = tile + pltpu.roll(tile, fold, 1)
    gram[0] = jnp.sum(jnp.where(mine, tile, 0.0), axis=0, keepdims=True)
    sum_copies = [
        pltpu.make_async_remote_copy(
            src_ref=gram.at[0],
            dst_ref=gram.at[dx * gy + dy],
            send_sem=sum_send.at[dx * gy + dy],
            recv_sem=sum_recv.at[dx * gy + dy],
            device_id=device(dx, dy),
            device_id_type=MESH,
        )
        for dx, dy in others
    ]
    for copy in sum_copies:
        copy.start()
    for copy in sum_copies:
        copy.wait_recv()
    row = gram[0]
    for n in range(1, gx * gy):
        row = row + gram[n]
    total = jnp.sum(jnp.where(mine, row, 0.0), axis=1, keepdims=True)
    moment = [total[n : n + 1, :] for n in range(2 * ITERS)]

    def inner(left, right):
        terms = [
            a * b * moment[i + j]
            for i, a in enumerate(left) for j, b in enumerate(right)
        ]
        return functools.reduce(lambda x, y: x + y, terms)

    def applied(poly):
        grown = poly + [jnp.zeros_like(poly[0])]
        return [grown[0]] + [grown[n] + grown[n - 1] for n in range(1, len(grown))]

    one = jnp.ones_like(moment[0])
    precond, direction, answer = [one], [one], []
    rz_now = inner(precond, precond)
    for step in range(ITERS):
        image = applied(direction)
        alpha = rz_now / inner(direction, image)
        answer = [
            (answer[n] if n < len(answer) else 0.0) + alpha * direction[n]
            for n in range(len(direction))
        ]
        if step + 1 < ITERS:
            precond = [
                (precond[n] if n < len(precond) else 0.0) - alpha * image[n]
                for n in range(len(image))
            ]
            rz_next = inner(precond, precond)
            beta = rz_next / rz_now
            direction = [
                precond[n] + (beta * direction[n] if n < len(direction) else 0.0)
                for n in range(len(precond))
            ]
            rz_now = rz_next
    pressure[...] = answer[0] * basis[0] + answer[1] * basis[1] + answer[2] * basis[2]

    for exchange in (level_copies, flow_copies, q_copies, forcing_copies):
        exchange.wait_send()
    for copy in flow_rows + q_rows + sum_copies:
        copy.wait_send()


def on_device(gx, gy, tracers, east_flow, north_flow, levels):
    pair, kl, rows, cols = tracers.shape
    planes = pair * kl
    ext = rows + 2 * HALO
    pad = rows + 2 * PAD
    f32 = jnp.float32
    in_hbm = pl.BlockSpec(memory_space=pltpu.HBM)
    plane = (kl, rows, cols)
    new_tracers, pressure = pl.pallas_call(
        functools.partial(fused, gx, gy),
        out_shape=(
            pltpu.VMEM((planes, rows, cols), f32),
            pltpu.VMEM((rows, cols), f32),
        ),
        in_specs=[in_hbm] * 4,
        out_specs=(pl.BlockSpec(memory_space=pltpu.VMEM),) * 2,
        scratch_shapes=[
            pltpu.VMEM((planes, pad, cols), f32),
            pltpu.VMEM((2, pad, cols), f32),
            pltpu.VMEM((2, pad, cols), f32),
            pltpu.VMEM(plane, jnp.bfloat16),
            pltpu.VMEM(plane, jnp.bfloat16),
            pltpu.VMEM((kl, pad, cols), f32),
            pltpu.VMEM((kl, pad, cols), f32),
            pltpu.VMEM((rows, cols), jnp.int32),
            pltpu.VMEM((3, pad, cols), jnp.bfloat16),
            pltpu.VMEM((5, pad, cols), f32),
            pltpu.VMEM((5, pad, cols), f32),
            pltpu.VMEM((5, ext, cols), f32),
            pltpu.VMEM((5, rows, cols), f32),
            pltpu.VMEM((6, ext, 2 * cols), f32),
            pltpu.VMEM((2, 4 * kl, cols), f32),
            pltpu.VMEM((2, 4 * kl, cols), f32),
            pltpu.VMEM((2, 2 * planes, cols), f32),
            pltpu.VMEM((2, 2 * planes, cols), f32),
            pltpu.VMEM((3, ext, cols), f32),
            pltpu.VMEM((3, ext, cols), f32),
            pltpu.VMEM((ext, cols), f32),
            pltpu.VMEM((ext, cols), f32),
            pltpu.VMEM((ext, cols), f32),
            pltpu.VMEM((2, ext, cols), f32),
            pltpu.VMEM((3, ext, cols), f32),
            pltpu.VMEM((8, cols), f32),
            pltpu.VMEM((gx * gy, 1, cols), f32),
            pltpu.SemaphoreType.DMA((3 + PIECES,)),
            pltpu.SemaphoreType.DMA((4, 8)),
            pltpu.SemaphoreType.DMA((4, 8)),
            pltpu.SemaphoreType.DMA((2, 2)),
            pltpu.SemaphoreType.DMA((2, 2)),
            pltpu.SemaphoreType.DMA((gx * gy,)),
            pltpu.SemaphoreType.DMA((gx * gy,)),
        ],
        compiler_params=pltpu.CompilerParams(
            collective_id=0, has_side_effects=True, vmem_limit_bytes=60 * 1024 * 1024
        ),
    )(tracers.reshape(planes, rows, cols), east_flow, north_flow, levels)
    return new_tracers.reshape(tracers.shape), pressure


def solution(mesh):
    placed = (P(None, None, "gx", "gy"), P(None, "gx", "gy"), P(None, "gx", "gy"), P("gx", "gy"))
    return jax.shard_map(
        functools.partial(on_device, mesh.shape["gx"], mesh.shape["gy"]),
        mesh=mesh,
        in_specs=placed,
        out_specs=(P(None, None, "gx", "gy"), P("gx", "gy")),
        check_vma=False,
    )
```

```python
import functools

import jax
import jax.numpy as jnp
from jax import lax
from jax.experimental import pallas as pl
from jax.experimental.pallas import tpu as pltpu
from jax.sharding import PartitionSpec as P

MESH = pl.DeviceIdType.MESH
ITERS = 3
KAPPA = 0.08
ALPHA = 0.05
HALO = 8
PAD = 16
PIECES = 4


def fused(
    gx, gy,
    tracers, east_flow, north_flow, levels,
    q2, pressure,
    q0, q1_a, q1_b, east_raw, north_raw, east_pad, north_pad, level_block, level_ext,
    coef_a, coef_b, reach, side_reach, operator_ext,
    flow_out, flow_in, row_out, row_in, flow_side, q_side, flow_join, east_join, q_join, q_swap,
    forcing_ext, gram_tile, gram,
    load_sem, ext_send, ext_recv, row_send, row_recv,
    sum_send, sum_recv,
):
    planes, rows, cols = tracers.shape
    kl = planes // 2
    top = HALO + rows
    ext = rows + 2 * HALO
    mx = lax.axis_index("gx")
    my = lax.axis_index("gy")
    own = pl.ds(HALO, rows)

    def device(dx, dy):
        return {"gx": lax.rem(mx + dx + gx, gx), "gy": lax.rem(my + dy + gy, gy)}

    loads = [
        pltpu.make_async_copy(levels, level_block, load_sem.at[0]),
        pltpu.make_async_copy(east_flow, east_raw, load_sem.at[1]),
        pltpu.make_async_copy(north_flow, north_raw, load_sem.at[2]),
    ]
    share = planes // PIECES
    for piece in range(PIECES):
        loads.append(
            pltpu.make_async_copy(
                tracers.at[pl.ds(piece * share, share)],
                q0.at[pl.ds(piece * share, share), pl.ds(PAD, rows)],
                load_sem.at[3 + piece],
            )
        )
    for load in loads[:3]:
        load.start()

    others = [(dx, dy) for dx in range(gx) for dy in range(gy) if (dx, dy) != (0, 0)]
    barrier = pltpu.get_barrier_semaphore()
    for dx, dy in others:
        pl.semaphore_signal(barrier, inc=1, device_id=device(dx, dy), device_id_type=MESH)

    has_north = my < gy - 1
    has_south = my > 0

    class Exchange:
        def __init__(self, buffer, which, rim, zonal=True):
            last, first, whole = pl.ds(rows, rim), pl.ds(rim, rim), pl.ds(rim, rows)
            low, high = pl.ds(0, rim), pl.ds(rim + rows, rim)
            plan = [
                (0, 1, whole, 2, whole), (0, -1, whole, 1, whole),
                (1, 1, last, 2, low), (-1, 1, first, 2, high),
                (1, -1, last, 1, low), (-1, -1, first, 1, high),
            ]
            if zonal:
                plan += [(1, 0, last, 0, low), (-1, 0, first, 0, high)]
            self.copies = [
                (
                    dy,
                    pltpu.make_async_remote_copy(
                        src_ref=buffer.at[0, source],
                        dst_ref=buffer.at[slot, place],
                        send_sem=ext_send.at[which, n],
                        recv_sem=ext_recv.at[which, n],
                        device_id=device(dx, dy),
                        device_id_type=MESH,
                    ),
                )
                for n, (dx, dy, source, slot, place) in enumerate(plan)
            ]

        def each(self, outward, action):
            for dy, copy in self.copies:
                if dy == 0:
                    action(copy)
                else:
                    pl.when(has_north if (dy > 0) == outward else has_south)(
                        functools.partial(action, copy)
                    )

        def start(self):
            self.each(True, lambda copy: copy.start())

        def wait_recv(self):
            self.each(False, lambda copy: copy.wait_recv())

        def wait_send(self):
            self.each(True, lambda copy: copy.wait_send())

    def row_copies(source, place, which):
        return [
            pltpu.make_async_remote_copy(
                src_ref=source.at[n],
                dst_ref=place.at[n],
                send_sem=row_send.at[which, n],
                recv_sem=row_recv.at[which, n],
                device_id=device(1 - 2 * n, 0),
                device_id_type=MESH,
            )
            for n in range(2)
        ]

    def lanes(count):
        return lax.broadcasted_iota(jnp.int32, (count, cols), 1)

    def row_of(ref, row):
        count, height, _ = ref.shape
        return ref.reshape(count * height, cols), pl.ds(row, count, stride=height)

    def rows_out(source, target, base, count):
        for n, first in ((0, PAD + rows - 2), (1, PAD)):
            for j in range(2):
                flat, place = row_of(source, first + j)
                target[n, pl.ds(base + j * count, count), :] = flat[place, :]

    def rows_in(source, target, base, count):
        for n, first in ((0, PAD - 2), (1, PAD + rows)):
            for j in range(2):
                flat, place = row_of(target, first + j)
                flat[place, :] = source[n, pl.ds(base + j * count, count), :]

    span = 32
    group = lanes(span) >> 2

    def put_side(target, r, pieces):
        place = pl.ds(HALO + r, span)
        total = target[0, place, :]
        for index, value in pieces:
            total = jnp.where(group == index, pltpu.roll(value, 4 * index + 2, 1), total)
        target[0, place, :] = total

    level_copies = Exchange(level_ext, 0, PAD)
    flow_copies = Exchange(flow_side, 1, HALO, zonal=False)
    q_copies = Exchange(q_side, 2, HALO, zonal=False)
    forcing_copies = Exchange(forcing_ext, 3, HALO)
    flow_rows = row_copies(flow_out, flow_in, 0)
    q_rows = row_copies(row_out, row_in, 1)
    flow_side[0] = jnp.zeros_like(flow_side[0])
    q_side[0] = jnp.zeros_like(q_side[0])
    loads[0].wait()
    level_ext[0, pl.ds(PAD, rows), :] = level_block[...].astype(jnp.float32).astype(jnp.bfloat16)
    pl.semaphore_wait(barrier, len(others))
    level_copies.start()
    loads[1].wait()
    loads[2].wait()
    for load in loads[3:]:
        load.start()

    def take_flow(g, carry):
        for r in range(0, rows, span):
            pieces = []
            for j in range(2):
                k = 2 * g + j
                east = east_raw[k, pl.ds(r, span), :].astype(jnp.float32)
                north = north_raw[k, pl.ds(r, span), :].astype(jnp.float32)
                east_pad[k, pl.ds(PAD + r, span), :] = east
                north_pad[k, pl.ds(PAD + r, span), :] = north
                pieces += [(k, east), (kl + k, north)]
            put_side(flow_side, r, pieces)
        return carry

    lax.fori_loop(0, kl // 2, take_flow, 0)
    rows_out(east_pad, flow_out, 0, kl)
    rows_out(north_pad, flow_out, 2 * kl, kl)
    flow_copies.start()
    for copy in flow_rows:
        copy.start()

    for load in loads[3:]:
        load.wait()
    bunch = 4

    def pack(g, carry):
        for r in range(0, rows, span):
            pieces = []
            for j in range(bunch):
                i = g * bunch + j
                pieces.append((i, q0[i, pl.ds(PAD + r, span), :]))
            put_side(q_side, r, pieces)
        return carry

    lax.fori_loop(0, planes // bunch, pack, 0)
    q_copies.start()
    rows_out(q0, row_out, 0, planes)
    for copy in q_rows:
        copy.start()

    level_copies.wait_recv()
    lane_ext = lanes(ext)
    north_lanes = jnp.where(has_north, cols, 0)
    south_lanes = jnp.where(has_south, cols, 0)

    def known(north, south, lane):
        return (
            jnp.where(lane < north_lanes, north, 0.0),
            jnp.where(lane < south_lanes, south, 0.0),
        )

    def join(parts):
        north, south = known(parts[1], parts[2], lane_ext)
        return jnp.concatenate(
            [parts[0], jnp.where(lane_ext < cols // 2, north, south)], axis=1
        )

    def neighbours(value):
        return (
            pltpu.roll(value, ext - 1, 0), pltpu.roll(value, 1, 0),
            pltpu.roll(value, 2 * cols - 1, 1), pltpu.roll(value, 1, 1),
        )

    trim = PAD - HALO
    depth = join(
        [level_ext[n].astype(jnp.float32)[trim : trim + ext] for n in range(3)]
    ) / kl
    sides = [jnp.minimum(depth, other) for other in neighbours(depth)]
    diagonal = ALPHA * depth + (depth == 0.0).astype(jnp.float32)
    diagonal = diagonal + sides[0] + sides[1] + sides[2] + sides[3]
    inverse = 1.0 / diagonal
    lane = lanes(rows)
    corner = lane & 3
    for n, side in enumerate(sides + [depth]):
        if n < 4:
            operator_ext[n] = -side * inverse
        scaled_side = side * kl
        reach[n] = scaled_side[:, :cols]
        edge = scaled_side[HALO:top, cols:]
        side_reach[n] = jnp.where(corner == 1, edge[:, cols - 1 : cols], edge[:, :1])
    operator_ext[4] = diagonal
    operator_ext[5] = inverse

    def merge(side):
        north, south = known(side[1], side[2], lane_ext)
        return jnp.where((lane_ext & 3) >= 2, north, south)

    def coefficients(level, limit, east, west, north, south):
        def gate(n, value):
            return jnp.where(level < limit(n), value, 0.0)

        def out_of(face):
            return jnp.maximum(face, 0.0) + KAPPA

        def back(face):
            return KAPPA - jnp.minimum(face, 0.0)

        lost = gate(0, out_of(east)) + gate(1, back(west)) + gate(2, out_of(north)) + gate(3, back(south))
        return (
            gate(4, 1.0 - lost), gate(0, back(east)), gate(1, out_of(west)),
            gate(2, back(north)), gate(3, out_of(south)),
        )

    flow_copies.wait_recv()
    for copy in flow_rows:
        copy.wait_recv()
    rows_in(flow_in, east_pad, 0, kl)
    rows_in(flow_in, north_pad, 2 * kl, kl)
    flow_join[...] = merge(flow_side)
    half = cols // 2
    joined = flow_join[...]
    turned = pltpu.roll(joined, half, 1)
    east_join[...] = jnp.where(lane_ext < half, joined, turned)
    north_side = jnp.where(lane_ext < half, turned, joined)[HALO:top]
    own_flow = flow_side[0, own, :]
    own_north = jnp.where(lane < half, pltpu.roll(own_flow, half, 1), own_flow)
    south_side = jnp.where(corner == 2, pltpu.roll(own_north, 1, 1), pltpu.roll(north_side, 1, 1))
    side_level = ((lane & (half - 1)) >> 2).astype(jnp.float32)
    side_coef = coefficients(
        side_level, lambda n: side_reach[n],
        east_join[own, :], east_join[pl.ds(HALO - 1, rows), :], north_side, south_side,
    )
    q_copies.wait_recv()
    q_join[...] = merge(q_side)
    here = q_join[own, :]
    own_side = q_side[0, own, :]
    north = jnp.where(corner == 1, pltpu.roll(own_side, cols - 1, 1), pltpu.roll(here, cols - 1, 1))
    south = jnp.where(corner == 2, pltpu.roll(own_side, 1, 1), pltpu.roll(here, 1, 1))
    moved = (
        side_coef[0] * here
        + side_coef[1] * q_join[pl.ds(HALO + 1, rows), :]
        + side_coef[2] * q_join[pl.ds(HALO - 1, rows), :]
        + side_coef[3] * north
        + side_coef[4] * south
    )

    def swap(value, place):
        return jnp.where((place & 3) == 1, pltpu.roll(value, cols - 1, 1), pltpu.roll(value, 1, 1))

    q_swap[0] = swap(q_join[...], lane_ext)
    q_swap[1, own, :] = swap(moved, lane)

    for copy in q_rows:
        copy.wait_recv()
    rows_in(row_in, q0, 0, planes)

    wide = 24
    lane_wide = lanes(wide)
    lane_span = lanes(span)
    forcing_ext[0, own, :] = jnp.zeros((rows, cols), jnp.float32)

    def advance(here, east, west, halo, coef, lane_here):
        north = jnp.where(lane_here == cols - 1, halo, pltpu.roll(here, cols - 1, 1))
        south = jnp.where(lane_here == 0, halo, pltpu.roll(here, 1, 1))
        return (
            coef[0] * here + coef[1] * east + coef[2] * west
            + coef[3] * north + coef[4] * south
        )

    def first_step(k, coef_ref, q_ref, e):
        part = pl.ds(e, wide)
        level = lax.convert_element_type(k, jnp.float32)
        east = east_pad[k, pl.ds(HALO + e, wide), :]
        north = north_pad[k, pl.ds(HALO + e, wide), :]
        halo = pltpu.roll(flow_join[part, :], cols // 2 - 1 - 4 * k, 1)
        south = jnp.where(lane_wide == 0, halo, pltpu.roll(north, 1, 1))

        def gated(n, face):
            is_open = level < reach[n, part, :]
            face = jnp.where(is_open, face, 0.0)
            out = jnp.maximum(face, 0.0) + jnp.where(is_open, KAPPA, 0.0)
            return out, out - face

        east_out, east_back = gated(0, east)
        coef_ref[1, pl.ds(HALO + e, wide), :] = east_back
        coef_ref[2, pl.ds(HALO + e, wide), :] = east_out
        north_out, north_back = gated(2, north)
        south_out, south_back = gated(3, south)
        west_back = coef_ref[1, pl.ds(HALO + e - 1, wide), :]
        west_out = coef_ref[2, pl.ds(HALO + e - 1, wide), :]
        lost = east_out + west_back + north_out + south_back
        centre = jnp.where(level < reach[4, part, :], 1.0 - lost, 0.0)
        coef = (centre, east_back, west_out, north_back, south_out)
        for n in (0, 3, 4):
            coef_ref[n, pl.ds(HALO + e, wide), :] = coef[n]
        for tracer in range(2):
            i = tracer * kl + k
            q_ref[tracer, pl.ds(HALO + e, wide), :] = advance(
                q0[i, pl.ds(HALO + e, wide), :],
                q0[i, pl.ds(HALO + e + 1, wide), :],
                q0[i, pl.ds(HALO + e - 1, wide), :],
                pltpu.roll(q_swap[0, part, :], cols - 2 - 4 * i, 1),
                coef, lane_wide,
            )

    def second_step(k, coef_ref, q_ref, r):
        part = pl.ds(HALO + r, span)
        coef = [coef_ref[n, pl.ds(PAD + r - (n == 2), span), :] for n in range(5)]
        result = []
        for tracer in range(2):
            i = tracer * kl + k
            value = advance(
                q_ref[tracer, pl.ds(PAD + r, span), :],
                q_ref[tracer, pl.ds(PAD + r + 1, span), :],
                q_ref[tracer, pl.ds(PAD + r - 1, span), :],
                pltpu.roll(q_swap[1, part, :], cols - 2 - 4 * i, 1),
                coef, lane_span,
            )
            q2[i, pl.ds(r, span), :] = value
            result.append(value)
        forcing_ext[0, part, :] += 0.25 * (result[0] - 0.8 * result[1])

    def beside(first, second):
        ahead = [functools.partial(first_step, *first, e) for e in range(0, ext, wide)] if first else []
        behind = [functools.partial(second_step, *second, r) for r in range(0, rows, span)] if second else []
        for n in range(max(len(ahead), len(behind))):
            for chunks in (ahead, behind):
                if n < len(chunks):
                    chunks[n]()

    slot_a, slot_b = (coef_a, q1_a), (coef_b, q1_b)
    beside((0, *slot_a), None)

    def two_levels(j, carry):
        k = 2 * j
        beside((k + 1, *slot_b), (k, *slot_a))
        beside((k + 2, *slot_a), (k + 1, *slot_b))
        return carry

    lax.fori_loop(0, kl // 2 - 1, two_levels, 0)
    beside((kl - 1, *slot_b), (kl - 2, *slot_a))
    beside(None, (kl - 1, *slot_b))
    forcing_copies.start()

    forcing_copies.wait_recv()
    basis = [join([forcing_ext[0], forcing_ext[1], forcing_ext[2]]) * operator_ext[5]]
    for step in range(ITERS):
        around = neighbours(basis[-1])
        basis.append(sum(operator_ext[n] * around[n] for n in range(4)))
    basis = [vector[HALO:top, :cols] for vector in basis]
    own_diagonal = operator_ext[4, pl.ds(HALO, rows), pl.ds(0, cols)]
    scaled = [own_diagonal * vector for vector in basis[:ITERS]]
    gram_tile[...] = jnp.zeros_like(gram_tile)
    for n in range(2 * ITERS):
        product = scaled[n // 2] * basis[(n + 1) // 2]
        gram_tile[pl.ds(n, 1), :] = jnp.sum(product, axis=0, keepdims=True)

    mine = (lanes(8) >> 4) == lax.broadcasted_iota(jnp.int32, (8, cols), 0)
    tile = gram_tile[...]
    for fold in (cols // 2, cols // 4, cols // 8):
        tile = tile + pltpu.roll(tile, fold, 1)
    gram[0] = jnp.sum(jnp.where(mine, tile, 0.0), axis=0, keepdims=True)
    sum_copies = [
        pltpu.make_async_remote_copy(
            src_ref=gram.at[0],
            dst_ref=gram.at[dx * gy + dy],
            send_sem=sum_send.at[dx * gy + dy],
            recv_sem=sum_recv.at[dx * gy + dy],
            device_id=device(dx, dy),
            device_id_type=MESH,
        )
        for dx, dy in others
    ]
    for copy in sum_copies:
        copy.start()
    for copy in sum_copies:
        copy.wait_recv()
    row = gram[0]
    for n in range(1, gx * gy):
        row = row + gram[n]
    total = jnp.sum(jnp.where(mine, row, 0.0), axis=1, keepdims=True)
    moment = [total[n : n + 1, :] for n in range(2 * ITERS)]

    def inner(left, right):
        terms = [
            a * b * moment[i + j]
            for i, a in enumerate(left) for j, b in enumerate(right)
        ]
        return functools.reduce(lambda x, y: x + y, terms)

    def applied(poly):
        grown = poly + [jnp.zeros_like(poly[0])]
        return [grown[0]] + [grown[n] + grown[n - 1] for n in range(1, len(grown))]

    one = jnp.ones_like(moment[0])
    precond, direction, answer = [one], [one], []
    rz_now = inner(precond, precond)
    for step in range(ITERS):
        image = applied(direction)
        alpha = rz_now / inner(direction, image)
        answer = [
            (answer[n] if n < len(answer) else 0.0) + alpha * direction[n]
            for n in range(len(direction))
        ]
        if step + 1 < ITERS:
            precond = [
                (precond[n] if n < len(precond) else 0.0) - alpha * image[n]
                for n in range(len(image))
            ]
            rz_next = inner(precond, precond)
            beta = rz_next / rz_now
            direction = [
                precond[n] + (beta * direction[n] if n < len(direction) else 0.0)
                for n in range(len(precond))
            ]
            rz_now = rz_next
    pressure[...] = answer[0] * basis[0] + answer[1] * basis[1] + answer[2] * basis[2]

    for exchange in (level_copies, flow_copies, q_copies, forcing_copies):
        exchange.wait_send()
    for copy in flow_rows + q_rows + sum_copies:
        copy.wait_send()


def hand_over(tracers, pressure, new_tracers, new_pressure, sem):
    share = tracers.shape[0] // PIECES
    copies = [pltpu.make_async_copy(pressure, new_pressure, sem.at[PIECES])]
    for piece in range(PIECES):
        part = pl.ds(piece * share, share)
        copies.append(pltpu.make_async_copy(tracers.at[part], new_tracers.at[part], sem.at[piece]))
    for copy in copies:
        copy.start()
    for copy in copies:
        copy.wait()


def on_device(gx, gy, tracers, east_flow, north_flow, levels):
    pair, kl, rows, cols = tracers.shape
    planes = pair * kl
    ext = rows + 2 * HALO
    pad = rows + 2 * PAD
    f32 = jnp.float32
    in_hbm = pl.BlockSpec(memory_space=pltpu.HBM)
    plane = (kl, rows, cols)
    new_tracers, pressure = pl.pallas_call(
        functools.partial(fused, gx, gy),
        out_shape=(
            pltpu.VMEM((planes, rows, cols), f32),
            pltpu.VMEM((rows, cols), f32),
        ),
        in_specs=[in_hbm] * 4,
        out_specs=(pl.BlockSpec(memory_space=pltpu.VMEM),) * 2,
        scratch_shapes=[
            pltpu.VMEM((planes, pad, cols), f32),
            pltpu.VMEM((2, pad, cols), f32),
            pltpu.VMEM((2, pad, cols), f32),
            pltpu.VMEM(plane, jnp.bfloat16),
            pltpu.VMEM(plane, jnp.bfloat16),
            pltpu.VMEM((kl, pad, cols), f32),
            pltpu.VMEM((kl, pad, cols), f32),
            pltpu.VMEM((rows, cols), jnp.int32),
            pltpu.VMEM((3, pad, cols), jnp.bfloat16),
            pltpu.VMEM((5, pad, cols), f32),
            pltpu.VMEM((5, pad, cols), f32),
            pltpu.VMEM((5, ext, cols), f32),
            pltpu.VMEM((5, rows, cols), f32),
            pltpu.VMEM((6, ext, 2 * cols), f32),
            pltpu.VMEM((2, 4 * kl, cols), f32),
            pltpu.VMEM((2, 4 * kl, cols), f32),
            pltpu.VMEM((2, 2 * planes, cols), f32),
            pltpu.VMEM((2, 2 * planes, cols), f32),
            pltpu.VMEM((3, ext, cols), f32),
            pltpu.VMEM((3, ext, cols), f32),
            pltpu.VMEM((ext, cols), f32),
            pltpu.VMEM((ext, cols), f32),
            pltpu.VMEM((ext, cols), f32),
            pltpu.VMEM((2, ext, cols), f32),
            pltpu.VMEM((3, ext, cols), f32),
            pltpu.VMEM((8, cols), f32),
            pltpu.VMEM((gx * gy, 1, cols), f32),
            pltpu.SemaphoreType.DMA((3 + PIECES,)),
            pltpu.SemaphoreType.DMA((4, 8)),
            pltpu.SemaphoreType.DMA((4, 8)),
            pltpu.SemaphoreType.DMA((2, 2)),
            pltpu.SemaphoreType.DMA((2, 2)),
            pltpu.SemaphoreType.DMA((gx * gy,)),
            pltpu.SemaphoreType.DMA((gx * gy,)),
        ],
        compiler_params=pltpu.CompilerParams(
            collective_id=0, has_side_effects=True, vmem_limit_bytes=60 * 1024 * 1024
        ),
    )(tracers.reshape(planes, rows, cols), east_flow, north_flow, levels)
    new_tracers, pressure = pl.pallas_call(
        hand_over,
        out_shape=(
            jax.ShapeDtypeStruct((planes, rows, cols), f32),
            jax.ShapeDtypeStruct((rows, cols), f32),
        ),
        in_specs=[pl.BlockSpec(memory_space=pltpu.VMEM)] * 2,
        out_specs=(in_hbm, in_hbm),
        scratch_shapes=[pltpu.SemaphoreType.DMA((PIECES + 1,))],
    )(new_tracers, pressure)
    return new_tracers.reshape(tracers.shape), pressure


def solution(mesh):
    placed = (P(None, None, "gx", "gy"), P(None, "gx", "gy"), P(None, "gx", "gy"), P("gx", "gy"))
    return jax.shard_map(
        functools.partial(on_device, mesh.shape["gx"], mesh.shape["gy"]),
        mesh=mesh,
        in_specs=placed,
        out_specs=(P(None, None, "gx", "gy"), P("gx", "gy")),
        check_vma=False,
    )
```

```python
import functools

import jax
import jax.numpy as jnp
from jax import lax
from jax.experimental import pallas as pl
from jax.experimental.pallas import tpu as pltpu
from jax.sharding import PartitionSpec as P

MESH = pl.DeviceIdType.MESH
ITERS = 3
KAPPA = 0.08
ALPHA = 0.05
HALO = 8
PAD = 16
PIECES = 4


def fused(
    gx, gy,
    tracers, east_flow, north_flow, levels,
    q2, pressure,
    q0, q1_a, q1_b, east_raw, north_raw, east_pad, north_pad, level_block, level_ext, level_rim,
    coef_a, coef_b, reach, side_reach, operator_ext,
    flow_out, flow_in, row_out, row_in, flow_side, q_side, flow_join, east_join, q_join, q_swap,
    forcing_ext, forcing_rim, gram_tile, gram,
    load_sem, ext_send, ext_recv, row_send, row_recv,
    sum_send, sum_recv,
):
    planes, rows, cols = tracers.shape
    kl = planes // 2
    top = HALO + rows
    ext = rows + 2 * HALO
    mx = lax.axis_index("gx")
    my = lax.axis_index("gy")
    own = pl.ds(HALO, rows)
    own_first = pl.ds(HALO, HALO)

    def device(dx, dy):
        return {"gx": lax.rem(mx + dx + gx, gx), "gy": lax.rem(my + dy + gy, gy)}

    loads = [
        pltpu.make_async_copy(levels, level_block, load_sem.at[0]),
        pltpu.make_async_copy(east_flow, east_raw, load_sem.at[1]),
        pltpu.make_async_copy(north_flow, north_raw, load_sem.at[2]),
    ]
    share = planes // PIECES
    for piece in range(PIECES):
        loads.append(
            pltpu.make_async_copy(
                tracers.at[pl.ds(piece * share, share)],
                q0.at[pl.ds(piece * share, share), pl.ds(PAD, rows)],
                load_sem.at[3 + piece],
            )
        )
    for load in loads:
        load.start()

    others = [(dx, dy) for dx in range(gx) for dy in range(gy) if (dx, dy) != (0, 0)]
    barrier = pltpu.get_barrier_semaphore()
    for dx, dy in others:
        pl.semaphore_signal(barrier, inc=1, device_id=device(dx, dy), device_id_type=MESH)

    has_north = my < gy - 1
    has_south = my > 0

    class Exchange:
        def __init__(self, buffer, which, zonal=None):
            count, rim = buffer.shape[1] - 2 * HALO, HALO
            last, first, whole = pl.ds(count, rim), pl.ds(rim, rim), pl.ds(rim, count)
            low, high = pl.ds(0, rim), pl.ds(rim + count, rim)
            plan = [
                (0, 1, whole, 2, whole), (0, -1, whole, 1, whole),
                (1, 1, last, 2, low), (-1, 1, first, 2, high),
                (1, -1, last, 1, low), (-1, -1, first, 1, high),
            ]
            self.copies = [
                (
                    dy,
                    pltpu.make_async_remote_copy(
                        src_ref=buffer.at[0, source],
                        dst_ref=buffer.at[slot, place],
                        send_sem=ext_send.at[which, n],
                        recv_sem=ext_recv.at[which, n],
                        device_id=device(dx, dy),
                        device_id_type=MESH,
                    ),
                )
                for n, (dx, dy, source, slot, place) in enumerate(plan)
            ]
            if zonal is not None:
                for n, (dx, source, place) in enumerate(
                    [(1, pl.ds(rows, HALO), pl.ds(0, HALO)), (-1, own_first, pl.ds(top, HALO))]
                ):
                    copy = pltpu.make_async_remote_copy(
                        src_ref=zonal.at[source],
                        dst_ref=zonal.at[place],
                        send_sem=ext_send.at[which, len(plan) + n],
                        recv_sem=ext_recv.at[which, len(plan) + n],
                        device_id=device(dx, 0),
                        device_id_type=MESH,
                    )
                    self.copies.append((0, copy))

        def each(self, outward, action):
            for dy, copy in self.copies:
                if dy == 0:
                    action(copy)
                else:
                    pl.when(has_north if (dy > 0) == outward else has_south)(
                        functools.partial(action, copy)
                    )

        def start(self):
            self.each(True, lambda copy: copy.start())

        def wait_recv(self):
            self.each(False, lambda copy: copy.wait_recv())

        def wait_send(self):
            self.each(True, lambda copy: copy.wait_send())

    def row_copies(source, place, which):
        return [
            pltpu.make_async_remote_copy(
                src_ref=source.at[n],
                dst_ref=place.at[n],
                send_sem=row_send.at[which, n],
                recv_sem=row_recv.at[which, n],
                device_id=device(1 - 2 * n, 0),
                device_id_type=MESH,
            )
            for n in range(2)
        ]

    def lanes(count):
        return lax.broadcasted_iota(jnp.int32, (count, cols), 1)

    def row_of(ref, row):
        count, height, _ = ref.shape
        return ref.reshape(count * height, cols), pl.ds(row, count, stride=height)

    def rows_out(source, target, base, count):
        for n, first in ((0, PAD + rows - 2), (1, PAD)):
            for j in range(2):
                flat, place = row_of(source, first + j)
                target[n, pl.ds(base + j * count, count), :] = flat[place, :]

    def rows_in(source, target, base, count):
        for n, first in ((0, PAD - 2), (1, PAD + rows)):
            for j in range(2):
                flat, place = row_of(target, first + j)
                flat[place, :] = source[n, pl.ds(base + j * count, count), :]

    span = 32
    group = lanes(span) >> 2

    def put_side(target, r, pieces):
        place = pl.ds(HALO + r, span)
        total = target[0, place, :]
        for index, value in pieces:
            total = jnp.where(group == index, pltpu.roll(value, 4 * index + 2, 1), total)
        target[0, place, :] = total

    level_copies = Exchange(level_rim, 0, level_ext)
    flow_copies = Exchange(flow_side, 1)
    q_copies = Exchange(q_side, 2)
    forcing_copies = Exchange(forcing_rim, 3, forcing_ext)
    flow_rows = row_copies(flow_out, flow_in, 0)
    q_rows = row_copies(row_out, row_in, 1)
    flow_side[0] = jnp.zeros_like(flow_side[0])
    q_side[0] = jnp.zeros_like(q_side[0])
    tall = 2 * HALO
    folds = rows // tall

    def fold_rim(source, rim):
        lane_tall = lanes(tall)
        total = jnp.zeros((tall, cols), jnp.float32)
        for c in range(folds):
            value = pltpu.roll(source[pl.ds(HALO + c * tall, tall), :], 8 * c + 4, 1)
            total = jnp.where(lane_tall >> 3 == c, value, total)
        rim[0, pl.ds(HALO, tall), :] = total

    def unfold_rim(rim):
        lane_rim = lanes(2 * tall)
        north, south = known(rim[1], rim[2], lane_rim)
        joint = jnp.where((lane_rim & 7) >= 4, north, south)

        def turn(value, c):
            return pltpu.roll(value, cols - 4 - 8 * c, 1)

        middle = joint[HALO : HALO + tall]
        parts = [turn(joint[:HALO], folds - 1)]
        parts += [turn(middle, c) for c in range(folds)]
        parts.append(turn(joint[HALO + tall :], 0))
        return jnp.concatenate(parts, axis=0)

    loads[0].wait()
    level_ext[own, :] = level_block[...].astype(jnp.float32)
    fold_rim(level_ext, level_rim)
    pl.semaphore_wait(barrier, len(others))
    level_copies.start()
    loads[1].wait()
    loads[2].wait()

    def take_flow(g, carry):
        for r in range(0, rows, span):
            pieces = []
            for j in range(2):
                k = 2 * g + j
                east = east_raw[k, pl.ds(r, span), :].astype(jnp.float32)
                north = north_raw[k, pl.ds(r, span), :].astype(jnp.float32)
                east_pad[k, pl.ds(PAD + r, span), :] = east
                north_pad[k, pl.ds(PAD + r, span), :] = north
                pieces += [(k, east), (kl + k, north)]
            put_side(flow_side, r, pieces)
        return carry

    lax.fori_loop(0, kl // 2, take_flow, 0)
    rows_out(east_pad, flow_out, 0, kl)
    rows_out(north_pad, flow_out, 2 * kl, kl)
    flow_copies.start()
    for copy in flow_rows:
        copy.start()

    for load in loads[3:]:
        load.wait()
    bunch = 4

    def pack(g, carry):
        for r in range(0, rows, span):
            pieces = []
            for j in range(bunch):
                i = g * bunch + j
                pieces.append((i, q0[i, pl.ds(PAD + r, span), :]))
            put_side(q_side, r, pieces)
        return carry

    lax.fori_loop(0, planes // bunch, pack, 0)
    q_copies.start()
    rows_out(q0, row_out, 0, planes)
    for copy in q_rows:
        copy.start()

    level_copies.wait_recv()
    lane_ext = lanes(ext)
    north_lanes = jnp.where(has_north, cols, 0)
    south_lanes = jnp.where(has_south, cols, 0)

    def known(north, south, lane):
        return (
            jnp.where(lane < north_lanes, north, 0.0),
            jnp.where(lane < south_lanes, south, 0.0),
        )

    def join(value, rim):
        return jnp.concatenate([value[...], unfold_rim(rim)], axis=1)

    def neighbours(value):
        return (
            pltpu.roll(value, ext - 1, 0), pltpu.roll(value, 1, 0),
            pltpu.roll(value, 2 * cols - 1, 1), pltpu.roll(value, 1, 1),
        )

    depth = join(level_ext, level_rim) / kl
    sides = [jnp.minimum(depth, other) for other in neighbours(depth)]
    diagonal = ALPHA * depth + (depth == 0.0).astype(jnp.float32)
    diagonal = diagonal + sides[0] + sides[1] + sides[2] + sides[3]
    inverse = 1.0 / diagonal
    lane = lanes(rows)
    corner = lane & 3
    for n, side in enumerate(sides + [depth]):
        if n < 4:
            operator_ext[n] = -side * inverse
        scaled_side = side * kl
        reach[n] = scaled_side[:, :cols]
        edge = scaled_side[HALO:top, cols:]
        side_reach[n] = jnp.where(corner == 1, edge[:, cols - 1 : cols], edge[:, :1])
    operator_ext[4] = diagonal
    operator_ext[5] = inverse

    def merge(side):
        north, south = known(side[1], side[2], lane_ext)
        return jnp.where((lane_ext & 3) >= 2, north, south)

    def coefficients(level, limit, east, west, north, south):
        def gate(n, value):
            return jnp.where(level < limit(n), value, 0.0)

        def out_of(face):
            return jnp.maximum(face, 0.0) + KAPPA

        def back(face):
            return KAPPA - jnp.minimum(face, 0.0)

        lost = gate(0, out_of(east)) + gate(1, back(west)) + gate(2, out_of(north)) + gate(3, back(south))
        return (
            gate(4, 1.0 - lost), gate(0, back(east)), gate(1, out_of(west)),
            gate(2, back(north)), gate(3, out_of(south)),
        )

    flow_copies.wait_recv()
    for copy in flow_rows:
        copy.wait_recv()
    rows_in(flow_in, east_pad, 0, kl)
    rows_in(flow_in, north_pad, 2 * kl, kl)
    flow_join[...] = merge(flow_side)
    half = cols // 2
    joined = flow_join[...]
    turned = pltpu.roll(joined, half, 1)
    east_join[...] = jnp.where(lane_ext < half, joined, turned)
    north_side = jnp.where(lane_ext < half, turned, joined)[HALO:top]
    own_flow = flow_side[0, own, :]
    own_north = jnp.where(lane < half, pltpu.roll(own_flow, half, 1), own_flow)
    south_side = jnp.where(corner == 2, pltpu.roll(own_north, 1, 1), pltpu.roll(north_side, 1, 1))
    side_level = ((lane & (half - 1)) >> 2).astype(jnp.float32)
    side_coef = coefficients(
        side_level, lambda n: side_reach[n],
        east_join[own, :], east_join[pl.ds(HALO - 1, rows), :], north_side, south_side,
    )
    q_copies.wait_recv()
    q_join[...] = merge(q_side)
    here = q_join[own, :]
    own_side = q_side[0, own, :]
    north = jnp.where(corner == 1, pltpu.roll(own_side, cols - 1, 1), pltpu.roll(here, cols - 1, 1))
    south = jnp.where(corner == 2, pltpu.roll(own_side, 1, 1), pltpu.roll(here, 1, 1))
    moved = (
        side_coef[0] * here
        + side_coef[1] * q_join[pl.ds(HALO + 1, rows), :]
        + side_coef[2] * q_join[pl.ds(HALO - 1, rows), :]
        + side_coef[3] * north
        + side_coef[4] * south
    )

    def swap(value, place):
        return jnp.where((place & 3) == 1, pltpu.roll(value, cols - 1, 1), pltpu.roll(value, 1, 1))

    q_swap[0] = swap(q_join[...], lane_ext)
    q_swap[1, own, :] = swap(moved, lane)

    for copy in q_rows:
        copy.wait_recv()
    rows_in(row_in, q0, 0, planes)

    wide = 24
    lane_wide = lanes(wide)
    lane_span = lanes(span)
    forcing_ext[own, :] = jnp.zeros((rows, cols), jnp.float32)

    def advance(here, east, west, halo, coef, lane_here):
        north = jnp.where(lane_here == cols - 1, halo, pltpu.roll(here, cols - 1, 1))
        south = jnp.where(lane_here == 0, halo, pltpu.roll(here, 1, 1))
        return (
            coef[0] * here + coef[1] * east + coef[2] * west
            + coef[3] * north + coef[4] * south
        )

    def first_step(k, coef_ref, q_ref, e):
        part = pl.ds(e, wide)
        level = lax.convert_element_type(k, jnp.float32)
        east = east_pad[k, pl.ds(HALO + e, wide), :]
        north = north_pad[k, pl.ds(HALO + e, wide), :]
        halo = pltpu.roll(flow_join[part, :], cols // 2 - 1 - 4 * k, 1)
        south = jnp.where(lane_wide == 0, halo, pltpu.roll(north, 1, 1))

        def gated(n, face):
            is_open = level < reach[n, part, :]
            face = jnp.where(is_open, face, 0.0)
            out = jnp.maximum(face, 0.0) + jnp.where(is_open, KAPPA, 0.0)
            return out, out - face

        east_out, east_back = gated(0, east)
        coef_ref[1, pl.ds(HALO + e, wide), :] = east_back
        coef_ref[2, pl.ds(HALO + e, wide), :] = east_out
        north_out, north_back = gated(2, north)
        south_out, south_back = gated(3, south)
        west_back = coef_ref[1, pl.ds(HALO + e - 1, wide), :]
        west_out = coef_ref[2, pl.ds(HALO + e - 1, wide), :]
        lost = east_out + west_back + north_out + south_back
        centre = jnp.where(level < reach[4, part, :], 1.0 - lost, 0.0)
        coef = (centre, east_back, west_out, north_back, south_out)
        for n in (0, 3, 4):
            coef_ref[n, pl.ds(HALO + e, wide), :] = coef[n]
        for tracer in range(2):
            i = tracer * kl + k
            q_ref[tracer, pl.ds(HALO + e, wide), :] = advance(
                q0[i, pl.ds(HALO + e, wide), :],
                q0[i, pl.ds(HALO + e + 1, wide), :],
                q0[i, pl.ds(HALO + e - 1, wide), :],
                pltpu.roll(q_swap[0, part, :], cols - 2 - 4 * i, 1),
                coef, lane_wide,
            )

    def second_step(k, coef_ref, q_ref, r):
        part = pl.ds(HALO + r, span)
        coef = [coef_ref[n, pl.ds(PAD + r - (n == 2), span), :] for n in range(5)]
        result = []
        for tracer in range(2):
            i = tracer * kl + k
            value = advance(
                q_ref[tracer, pl.ds(PAD + r, span), :],
                q_ref[tracer, pl.ds(PAD + r + 1, span), :],
                q_ref[tracer, pl.ds(PAD + r - 1, span), :],
                pltpu.roll(q_swap[1, part, :], cols - 2 - 4 * i, 1),
                coef, lane_span,
            )
            q2[i, pl.ds(r, span), :] = value
            result.append(value)
        forcing_ext[part, :] += 0.25 * (result[0] - 0.8 * result[1])

    def beside(first, second):
        ahead = [functools.partial(first_step, *first, e) for e in range(0, ext, wide)] if first else []
        behind = [functools.partial(second_step, *second, r) for r in range(0, rows, span)] if second else []
        for n in range(max(len(ahead), len(behind))):
            for chunks in (ahead, behind):
                if n < len(chunks):
                    chunks[n]()

    slot_a, slot_b = (coef_a, q1_a), (coef_b, q1_b)
    beside((0, *slot_a), None)

    def two_levels(j, carry):
        k = 2 * j
        beside((k + 1, *slot_b), (k, *slot_a))
        beside((k + 2, *slot_a), (k + 1, *slot_b))
        return carry

    lax.fori_loop(0, kl // 2 - 1, two_levels, 0)
    beside((kl - 1, *slot_b), (kl - 2, *slot_a))
    beside(None, (kl - 1, *slot_b))
    fold_rim(forcing_ext, forcing_rim)
    forcing_copies.start()

    forcing_copies.wait_recv()
    basis = [join(forcing_ext, forcing_rim) * operator_ext[5]]
    for step in range(ITERS):
        around = neighbours(basis[-1])
        basis.append(sum(operator_ext[n] * around[n] for n in range(4)))
    basis = [vector[HALO:top, :cols] for vector in basis]
    own_diagonal = operator_ext[4, pl.ds(HALO, rows), pl.ds(0, cols)]
    scaled = [own_diagonal * vector for vector in basis[:ITERS]]
    gram_tile[...] = jnp.zeros_like(gram_tile)
    for n in range(2 * ITERS):
        product = scaled[n // 2] * basis[(n + 1) // 2]
        gram_tile[pl.ds(n, 1), :] = jnp.sum(product, axis=0, keepdims=True)

    mine = (lanes(8) >> 4) == lax.broadcasted_iota(jnp.int32, (8, cols), 0)
    tile = gram_tile[...]
    for fold in (cols // 2, cols // 4, cols // 8):
        tile = tile + pltpu.roll(tile, fold, 1)
    gram[0] = jnp.sum(jnp.where(mine, tile, 0.0), axis=0, keepdims=True)
    sum_copies = [
        pltpu.make_async_remote_copy(
            src_ref=gram.at[0],
            dst_ref=gram.at[dx * gy + dy],
            send_sem=sum_send.at[dx * gy + dy],
            recv_sem=sum_recv.at[dx * gy + dy],
            device_id=device(dx, dy),
            device_id_type=MESH,
        )
        for dx, dy in others
    ]
    for copy in sum_copies:
        copy.start()
    for copy in sum_copies:
        copy.wait_recv()
    row = gram[0]
    for n in range(1, gx * gy):
        row = row + gram[n]
    total = jnp.sum(jnp.where(mine, row, 0.0), axis=1, keepdims=True)
    moment = [total[n : n + 1, :] for n in range(2 * ITERS)]

    def inner(left, right):
        terms = [
            a * b * moment[i + j]
            for i, a in enumerate(left) for j, b in enumerate(right)
        ]
        return functools.reduce(lambda x, y: x + y, terms)

    def applied(poly):
        grown = poly + [jnp.zeros_like(poly[0])]
        return [grown[0]] + [grown[n] + grown[n - 1] for n in range(1, len(grown))]

    one = jnp.ones_like(moment[0])
    precond, direction, answer = [one], [one], []
    rz_now = inner(precond, precond)
    for step in range(ITERS):
        image = applied(direction)
        alpha = rz_now / inner(direction, image)
        answer = [
            (answer[n] if n < len(answer) else 0.0) + alpha * direction[n]
            for n in range(len(direction))
        ]
        if step + 1 < ITERS:
            precond = [
                (precond[n] if n < len(precond) else 0.0) - alpha * image[n]
                for n in range(len(image))
            ]
            rz_next = inner(precond, precond)
            beta = rz_next / rz_now
            direction = [
                precond[n] + (beta * direction[n] if n < len(direction) else 0.0)
                for n in range(len(precond))
            ]
            rz_now = rz_next
    pressure[...] = answer[0] * basis[0] + answer[1] * basis[1] + answer[2] * basis[2]

    for exchange in (level_copies, flow_copies, q_copies, forcing_copies):
        exchange.wait_send()
    for copy in flow_rows + q_rows + sum_copies:
        copy.wait_send()


def on_device(gx, gy, tracers, east_flow, north_flow, levels):
    pair, kl, rows, cols = tracers.shape
    planes = pair * kl
    ext = rows + 2 * HALO
    pad = rows + 2 * PAD
    f32 = jnp.float32
    in_hbm = pl.BlockSpec(memory_space=pltpu.HBM)
    plane = (kl, rows, cols)
    new_tracers, pressure = pl.pallas_call(
        functools.partial(fused, gx, gy),
        out_shape=(
            pltpu.VMEM((planes, rows, cols), f32),
            pltpu.VMEM((rows, cols), f32),
        ),
        in_specs=[in_hbm] * 4,
        out_specs=(pl.BlockSpec(memory_space=pltpu.VMEM),) * 2,
        scratch_shapes=[
            pltpu.VMEM((planes, pad, cols), f32),
            pltpu.VMEM((2, pad, cols), f32),
            pltpu.VMEM((2, pad, cols), f32),
            pltpu.VMEM(plane, jnp.bfloat16),
            pltpu.VMEM(plane, jnp.bfloat16),
            pltpu.VMEM((kl, pad, cols), f32),
            pltpu.VMEM((kl, pad, cols), f32),
            pltpu.VMEM((rows, cols), jnp.int32),
            pltpu.VMEM((ext, cols), f32),
            pltpu.VMEM((3, 4 * HALO, cols), f32),
            pltpu.VMEM((5, pad, cols), f32),
            pltpu.VMEM((5, pad, cols), f32),
            pltpu.VMEM((5, ext, cols), f32),
            pltpu.VMEM((5, rows, cols), f32),
            pltpu.VMEM((6, ext, 2 * cols), f32),
            pltpu.VMEM((2, 4 * kl, cols), f32),
            pltpu.VMEM((2, 4 * kl, cols), f32),
            pltpu.VMEM((2, 2 * planes, cols), f32),
            pltpu.VMEM((2, 2 * planes, cols), f32),
            pltpu.VMEM((3, ext, cols), f32),
            pltpu.VMEM((3, ext, cols), f32),
            pltpu.VMEM((ext, cols), f32),
            pltpu.VMEM((ext, cols), f32),
            pltpu.VMEM((ext, cols), f32),
            pltpu.VMEM((2, ext, cols), f32),
            pltpu.VMEM((ext, cols), f32),
            pltpu.VMEM((3, 4 * HALO, cols), f32),
            pltpu.VMEM((8, cols), f32),
            pltpu.VMEM((gx * gy, 1, cols), f32),
            pltpu.SemaphoreType.DMA((3 + PIECES,)),
            pltpu.SemaphoreType.DMA((4, 8)),
            pltpu.SemaphoreType.DMA((4, 8)),
            pltpu.SemaphoreType.DMA((2, 2)),
            pltpu.SemaphoreType.DMA((2, 2)),
            pltpu.SemaphoreType.DMA((gx * gy,)),
            pltpu.SemaphoreType.DMA((gx * gy,)),
        ],
        compiler_params=pltpu.CompilerParams(
            collective_id=0, has_side_effects=True, vmem_limit_bytes=60 * 1024 * 1024
        ),
    )(tracers.reshape(planes, rows, cols), east_flow, north_flow, levels)
    return new_tracers.reshape(tracers.shape), pressure


def solution(mesh):
    placed = (P(None, None, "gx", "gy"), P(None, "gx", "gy"), P(None, "gx", "gy"), P("gx", "gy"))
    return jax.shard_map(
        functools.partial(on_device, mesh.shape["gx"], mesh.shape["gy"]),
        mesh=mesh,
        in_specs=placed,
        out_specs=(P(None, None, "gx", "gy"), P("gx", "gy")),
        check_vma=False,
    )
```

```python
import functools

import jax
import jax.numpy as jnp
from jax import lax
from jax.experimental import pallas as pl
from jax.experimental.pallas import tpu as pltpu
from jax.sharding import PartitionSpec as P

MESH = pl.DeviceIdType.MESH
ITERS = 3
KAPPA = 0.08
ALPHA = 0.05
HALO = 8
PAD = 16
PIECES = 4


def fused(
    gx, gy,
    tracers, east_flow, north_flow, levels,
    q2, pressure,
    q0, q1_a, q1_b, east_raw, north_raw, east_pad, north_pad, level_block, level_ext,
    coef_a, coef_b, reach, side_reach, operator_ext,
    flow_out, flow_in, row_out, row_in, flow_side, q_side, flow_join, east_join, q_join, q_swap,
    forcing_ext, gram_tile, gram,
    load_sem, ext_send, ext_recv, row_send, row_recv,
    sum_send, sum_recv,
):
    planes, rows, cols = tracers.shape
    kl = planes // 2
    top = HALO + rows
    ext = rows + 2 * HALO
    mx = lax.axis_index("gx")
    my = lax.axis_index("gy")
    own = pl.ds(HALO, rows)

    def device(dx, dy):
        return {"gx": lax.rem(mx + dx + gx, gx), "gy": lax.rem(my + dy + gy, gy)}

    loads = [
        pltpu.make_async_copy(levels, level_block, load_sem.at[0]),
        pltpu.make_async_copy(east_flow, east_raw, load_sem.at[1]),
        pltpu.make_async_copy(north_flow, north_raw, load_sem.at[2]),
    ]
    share = planes // PIECES
    for piece in range(PIECES):
        loads.append(
            pltpu.make_async_copy(
                tracers.at[pl.ds(piece * share, share)],
                q0.at[pl.ds(piece * share, share), pl.ds(PAD, rows)],
                load_sem.at[3 + piece],
            )
        )
    for load in loads:
        load.start()

    along_x = [(dx, 0) for dx in range(1, gx)]
    along_y = [(0, dy) for dy in range(1, gy)]
    others = along_x + along_y + [(1, 1), (1, -1), (-1, 1), (-1, -1)]
    barrier = pltpu.get_barrier_semaphore()
    for dx, dy in others:
        pl.semaphore_signal(barrier, inc=1, device_id=device(dx, dy), device_id_type=MESH)

    has_north = my < gy - 1
    has_south = my > 0

    class Exchange:
        def __init__(self, buffer, which, rim, zonal=True):
            last, first, whole = pl.ds(rows, rim), pl.ds(rim, rim), pl.ds(rim, rows)
            low, high = pl.ds(0, rim), pl.ds(rim + rows, rim)
            plan = [
                (0, 1, whole, 2, whole), (0, -1, whole, 1, whole),
                (1, 1, last, 2, low), (-1, 1, first, 2, high),
                (1, -1, last, 1, low), (-1, -1, first, 1, high),
            ]
            if zonal:
                plan += [(1, 0, last, 0, low), (-1, 0, first, 0, high)]
            self.copies = [
                (
                    dy,
                    pltpu.make_async_remote_copy(
                        src_ref=buffer.at[0, source],
                        dst_ref=buffer.at[slot, place],
                        send_sem=ext_send.at[which, n],
                        recv_sem=ext_recv.at[which, n],
                        device_id=device(dx, dy),
                        device_id_type=MESH,
                    ),
                )
                for n, (dx, dy, source, slot, place) in enumerate(plan)
            ]

        def each(self, outward, action):
            for dy, copy in self.copies:
                if dy == 0:
                    action(copy)
                else:
                    pl.when(has_north if (dy > 0) == outward else has_south)(
                        functools.partial(action, copy)
                    )

        def start(self):
            self.each(True, lambda copy: copy.start())

        def wait_recv(self):
            self.each(False, lambda copy: copy.wait_recv())

        def wait_send(self):
            self.each(True, lambda copy: copy.wait_send())

    def row_copies(source, place, which):
        return [
            pltpu.make_async_remote_copy(
                src_ref=source.at[n],
                dst_ref=place.at[n],
                send_sem=row_send.at[which, n],
                recv_sem=row_recv.at[which, n],
                device_id=device(1 - 2 * n, 0),
                device_id_type=MESH,
            )
            for n in range(2)
        ]

    def lanes(count):
        return lax.broadcasted_iota(jnp.int32, (count, cols), 1)

    def row_of(ref, row):
        count, height, _ = ref.shape
        return ref.reshape(count * height, cols), pl.ds(row, count, stride=height)

    def rows_out(source, target, base, count):
        for n, first in ((0, PAD + rows - 2), (1, PAD)):
            for j in range(2):
                flat, place = row_of(source, first + j)
                target[n, pl.ds(base + j * count, count), :] = flat[place, :]

    def rows_in(source, target, base, count):
        for n, first in ((0, PAD - 2), (1, PAD + rows)):
            for j in range(2):
                flat, place = row_of(target, first + j)
                flat[place, :] = source[n, pl.ds(base + j * count, count), :]

    span = 32
    group = lanes(span) >> 2

    def put_side(target, r, pieces):
        place = pl.ds(HALO + r, span)
        total = target[0, place, :]
        for index, value in pieces:
            total = jnp.where(group == index, pltpu.roll(value, 4 * index + 2, 1), total)
        target[0, place, :] = total

    level_copies = Exchange(level_ext, 0, PAD)
    flow_copies = Exchange(flow_side, 1, HALO, zonal=False)
    q_copies = Exchange(q_side, 2, HALO, zonal=False)
    forcing_copies = Exchange(forcing_ext, 3, HALO)
    flow_rows = row_copies(flow_out, flow_in, 0)
    q_rows = row_copies(row_out, row_in, 1)
    flow_side[0] = jnp.zeros_like(flow_side[0])
    q_side[0] = jnp.zeros_like(q_side[0])
    loads[0].wait()
    level_ext[0, pl.ds(PAD, rows), :] = level_block[...].astype(jnp.float32).astype(jnp.bfloat16)
    pl.semaphore_wait(barrier, len(others))
    level_copies.start()
    loads[1].wait()
    loads[2].wait()

    def take_flow(g, carry):
        for r in range(0, rows, span):
            pieces = []
            for j in range(2):
                k = 2 * g + j
                east = east_raw[k, pl.ds(r, span), :].astype(jnp.float32)
                north = north_raw[k, pl.ds(r, span), :].astype(jnp.float32)
                east_pad[k, pl.ds(PAD + r, span), :] = east
                north_pad[k, pl.ds(PAD + r, span), :] = north
                pieces += [(k, east), (kl + k, north)]
            put_side(flow_side, r, pieces)
        return carry

    lax.fori_loop(0, kl // 2, take_flow, 0)
    rows_out(east_pad, flow_out, 0, kl)
    rows_out(north_pad, flow_out, 2 * kl, kl)
    flow_copies.start()
    for copy in flow_rows:
        copy.start()

    for load in loads[3:]:
        load.wait()
    bunch = 4

    def pack(g, carry):
        for r in range(0, rows, span):
            pieces = []
            for j in range(bunch):
                i = g * bunch + j
                pieces.append((i, q0[i, pl.ds(PAD + r, span), :]))
            put_side(q_side, r, pieces)
        return carry

    lax.fori_loop(0, planes // bunch, pack, 0)
    q_copies.start()
    rows_out(q0, row_out, 0, planes)
    for copy in q_rows:
        copy.start()

    level_copies.wait_recv()
    lane_ext = lanes(ext)
    north_lanes = jnp.where(has_north, cols, 0)
    south_lanes = jnp.where(has_south, cols, 0)

    def known(north, south, lane):
        return (
            jnp.where(lane < north_lanes, north, 0.0),
            jnp.where(lane < south_lanes, south, 0.0),
        )

    def join(parts):
        north, south = known(parts[1], parts[2], lane_ext)
        return jnp.concatenate(
            [parts[0], jnp.where(lane_ext < cols // 2, north, south)], axis=1
        )

    def neighbours(value):
        return (
            pltpu.roll(value, ext - 1, 0), pltpu.roll(value, 1, 0),
            pltpu.roll(value, 2 * cols - 1, 1), pltpu.roll(value, 1, 1),
        )

    trim = PAD - HALO
    depth = join(
        [level_ext[n].astype(jnp.float32)[trim : trim + ext] for n in range(3)]
    ) / kl
    sides = [jnp.minimum(depth, other) for other in neighbours(depth)]
    diagonal = ALPHA * depth + (depth == 0.0).astype(jnp.float32)
    diagonal = diagonal + sides[0] + sides[1] + sides[2] + sides[3]
    inverse = 1.0 / diagonal
    lane = lanes(rows)
    corner = lane & 3
    for n, side in enumerate(sides + [depth]):
        if n < 4:
            operator_ext[n] = -side * inverse
        scaled_side = side * kl
        reach[n] = scaled_side[:, :cols]
        edge = scaled_side[HALO:top, cols:]
        side_reach[n] = jnp.where(corner == 1, edge[:, cols - 1 : cols], edge[:, :1])
    operator_ext[4] = diagonal
    operator_ext[5] = inverse

    def merge(side):
        north, south = known(side[1], side[2], lane_ext)
        return jnp.where((lane_ext & 3) >= 2, north, south)

    def coefficients(level, limit, east, west, north, south):
        def gate(n, value):
            return jnp.where(level < limit(n), value, 0.0)

        def out_of(face):
            return jnp.maximum(face, 0.0) + KAPPA

        def back(face):
            return KAPPA - jnp.minimum(face, 0.0)

        lost = gate(0, out_of(east)) + gate(1, back(west)) + gate(2, out_of(north)) + gate(3, back(south))
        return (
            gate(4, 1.0 - lost), gate(0, back(east)), gate(1, out_of(west)),
            gate(2, back(north)), gate(3, out_of(south)),
        )

    flow_copies.wait_recv()
    for copy in flow_rows:
        copy.wait_recv()
    rows_in(flow_in, east_pad, 0, kl)
    rows_in(flow_in, north_pad, 2 * kl, kl)
    flow_join[...] = merge(flow_side)
    half = cols // 2
    joined = flow_join[...]
    turned = pltpu.roll(joined, half, 1)
    east_join[...] = jnp.where(lane_ext < half, joined, turned)
    north_side = jnp.where(lane_ext < half, turned, joined)[HALO:top]
    own_flow = flow_side[0, own, :]
    own_north = jnp.where(lane < half, pltpu.roll(own_flow, half, 1), own_flow)
    south_side = jnp.where(corner == 2, pltpu.roll(own_north, 1, 1), pltpu.roll(north_side, 1, 1))
    side_level = ((lane & (half - 1)) >> 2).astype(jnp.float32)
    side_coef = coefficients(
        side_level, lambda n: side_reach[n],
        east_join[own, :], east_join[pl.ds(HALO - 1, rows), :], north_side, south_side,
    )
    q_copies.wait_recv()
    q_join[...] = merge(q_side)
    here = q_join[own, :]
    own_side = q_side[0, own, :]
    north = jnp.where(corner == 1, pltpu.roll(own_side, cols - 1, 1), pltpu.roll(here, cols - 1, 1))
    south = jnp.where(corner == 2, pltpu.roll(own_side, 1, 1), pltpu.roll(here, 1, 1))
    moved = (
        side_coef[0] * here
        + side_coef[1] * q_join[pl.ds(HALO + 1, rows), :]
        + side_coef[2] * q_join[pl.ds(HALO - 1, rows), :]
        + side_coef[3] * north
        + side_coef[4] * south
    )

    def swap(value, place):
        return jnp.where((place & 3) == 1, pltpu.roll(value, cols - 1, 1), pltpu.roll(value, 1, 1))

    q_swap[0] = swap(q_join[...], lane_ext)
    q_swap[1, own, :] = swap(moved, lane)

    for copy in q_rows:
        copy.wait_recv()
    rows_in(row_in, q0, 0, planes)

    wide = 24
    lane_wide = lanes(wide)
    lane_span = lanes(span)
    forcing_ext[0, own, :] = jnp.zeros((rows, cols), jnp.float32)

    def advance(here, east, west, halo, coef, lane_here):
        north = jnp.where(lane_here == cols - 1, halo, pltpu.roll(here, cols - 1, 1))
        south = jnp.where(lane_here == 0, halo, pltpu.roll(here, 1, 1))
        return (
            coef[0] * here + coef[1] * east + coef[2] * west
            + coef[3] * north + coef[4] * south
        )

    def first_step(k, coef_ref, q_ref, e):
        part = pl.ds(e, wide)
        level = lax.convert_element_type(k, jnp.float32)
        east = east_pad[k, pl.ds(HALO + e, wide), :]
        north = north_pad[k, pl.ds(HALO + e, wide), :]
        halo = pltpu.roll(flow_join[part, :], cols // 2 - 1 - 4 * k, 1)
        south = jnp.where(lane_wide == 0, halo, pltpu.roll(north, 1, 1))

        def gated(n, face):
            is_open = level < reach[n, part, :]
            face = jnp.where(is_open, face, 0.0)
            out = jnp.maximum(face, 0.0) + jnp.where(is_open, KAPPA, 0.0)
            return out, out - face

        east_out, east_back = gated(0, east)
        coef_ref[1, pl.ds(HALO + e, wide), :] = east_back
        coef_ref[2, pl.ds(HALO + e, wide), :] = east_out
        north_out, north_back = gated(2, north)
        south_out, south_back = gated(3, south)
        west_back = coef_ref[1, pl.ds(HALO + e - 1, wide), :]
        west_out = coef_ref[2, pl.ds(HALO + e - 1, wide), :]
        lost = east_out + west_back + north_out + south_back
        centre = jnp.where(level < reach[4, part, :], 1.0 - lost, 0.0)
        coef = (centre, east_back, west_out, north_back, south_out)
        for n in (0, 3, 4):
            coef_ref[n, pl.ds(HALO + e, wide), :] = coef[n]
        for tracer in range(2):
            i = tracer * kl + k
            q_ref[tracer, pl.ds(HALO + e, wide), :] = advance(
                q0[i, pl.ds(HALO + e, wide), :],
                q0[i, pl.ds(HALO + e + 1, wide), :],
                q0[i, pl.ds(HALO + e - 1, wide), :],
                pltpu.roll(q_swap[0, part, :], cols - 2 - 4 * i, 1),
                coef, lane_wide,
            )

    def second_step(k, coef_ref, q_ref, r):
        part = pl.ds(HALO + r, span)
        coef = [coef_ref[n, pl.ds(PAD + r - (n == 2), span), :] for n in range(5)]
        result = []
        for tracer in range(2):
            i = tracer * kl + k
            value = advance(
                q_ref[tracer, pl.ds(PAD + r, span), :],
                q_ref[tracer, pl.ds(PAD + r + 1, span), :],
                q_ref[tracer, pl.ds(PAD + r - 1, span), :],
                pltpu.roll(q_swap[1, part, :], cols - 2 - 4 * i, 1),
                coef, lane_span,
            )
            q2[i, pl.ds(r, span), :] = value
            result.append(value)
        forcing_ext[0, part, :] += 0.25 * (result[0] - 0.8 * result[1])

    def beside(first, second):
        ahead = [functools.partial(first_step, *first, e) for e in range(0, ext, wide)] if first else []
        behind = [functools.partial(second_step, *second, r) for r in range(0, rows, span)] if second else []
        for n in range(max(len(ahead), len(behind))):
            for chunks in (ahead, behind):
                if n < len(chunks):
                    chunks[n]()

    slot_a, slot_b = (coef_a, q1_a), (coef_b, q1_b)
    beside((0, *slot_a), None)

    def two_levels(j, carry):
        k = 2 * j
        beside((k + 1, *slot_b), (k, *slot_a))
        beside((k + 2, *slot_a), (k + 1, *slot_b))
        return carry

    lax.fori_loop(0, kl // 2 - 1, two_levels, 0)
    beside((kl - 1, *slot_b), (kl - 2, *slot_a))
    beside(None, (kl - 1, *slot_b))
    forcing_copies.start()
    for exchange in (level_copies, flow_copies, q_copies):
        exchange.wait_send()
    for copy in flow_rows + q_rows:
        copy.wait_send()

    forcing_copies.wait_recv()
    basis = [join([forcing_ext[0], forcing_ext[1], forcing_ext[2]]) * operator_ext[5]]
    for step in range(ITERS):
        around = neighbours(basis[-1])
        basis.append(sum(operator_ext[n] * around[n] for n in range(4)))
    basis = [vector[HALO:top, :cols] for vector in basis]
    own_diagonal = operator_ext[4, pl.ds(HALO, rows), pl.ds(0, cols)]
    scaled = [own_diagonal * vector for vector in basis[:ITERS]]
    gram_tile[...] = jnp.zeros_like(gram_tile)
    for n in range(2 * ITERS):
        product = scaled[n // 2] * basis[(n + 1) // 2]
        gram_tile[pl.ds(n, 1), :] = jnp.sum(product, axis=0, keepdims=True)

    mine = (lanes(8) >> 4) == lax.broadcasted_iota(jnp.int32, (8, cols), 0)
    tile = gram_tile[...]
    for fold in (cols // 2, cols // 4, cols // 8):
        tile = tile + pltpu.roll(tile, fold, 1)
    gram[0] = jnp.sum(jnp.where(mine, tile, 0.0), axis=0, keepdims=True)

    def spread(base, targets):
        copies = [
            pltpu.make_async_remote_copy(
                src_ref=gram.at[base],
                dst_ref=gram.at[base + dx + dy],
                send_sem=sum_send.at[base + dx + dy],
                recv_sem=sum_recv.at[base + dx + dy],
                device_id=device(dx, dy),
                device_id_type=MESH,
            )
            for dx, dy in targets
        ]
        for copy in copies:
            copy.start()
        return copies

    def gather(base, copies):
        for copy in copies:
            copy.wait_recv()
        row = gram[base]
        for n in range(1, len(copies) + 1):
            row = row + gram[base + n]
        return row

    y_copies = spread(0, along_y)
    forcing_copies.wait_send()
    gram[gy] = gather(0, y_copies)
    x_copies = spread(gy, along_x)
    sum_copies = y_copies + x_copies
    row = gather(gy, x_copies)
    total = jnp.sum(jnp.where(mine, row, 0.0), axis=1, keepdims=True)
    moment = [total[n : n + 1, :] for n in range(2 * ITERS)]

    def inner(left, right):
        terms = [
            a * b * moment[i + j]
            for i, a in enumerate(left) for j, b in enumerate(right)
        ]
        return functools.reduce(lambda x, y: x + y, terms)

    def applied(poly):
        grown = poly + [jnp.zeros_like(poly[0])]
        return [grown[0]] + [grown[n] + grown[n - 1] for n in range(1, len(grown))]

    one = jnp.ones_like(moment[0])
    precond, direction, answer = [one], [one], []
    rz_now = inner(precond, precond)
    for step in range(ITERS):
        image = applied(direction)
        alpha = rz_now / inner(direction, image)
        answer = [
            (answer[n] if n < len(answer) else 0.0) + alpha * direction[n]
            for n in range(len(direction))
        ]
        if step + 1 < ITERS:
            precond = [
                (precond[n] if n < len(precond) else 0.0) - alpha * image[n]
                for n in range(len(image))
            ]
            rz_next = inner(precond, precond)
            beta = rz_next / rz_now
            direction = [
                precond[n] + (beta * direction[n] if n < len(direction) else 0.0)
                for n in range(len(precond))
            ]
            rz_now = rz_next
    pressure[...] = answer[0] * basis[0] + answer[1] * basis[1] + answer[2] * basis[2]

    for copy in sum_copies:
        copy.wait_send()


def on_device(gx, gy, tracers, east_flow, north_flow, levels):
    pair, kl, rows, cols = tracers.shape
    planes = pair * kl
    ext = rows + 2 * HALO
    pad = rows + 2 * PAD
    f32 = jnp.float32
    in_hbm = pl.BlockSpec(memory_space=pltpu.HBM)
    plane = (kl, rows, cols)
    new_tracers, pressure = pl.pallas_call(
        functools.partial(fused, gx, gy),
        out_shape=(
            pltpu.VMEM((planes, rows, cols), f32),
            pltpu.VMEM((rows, cols), f32),
        ),
        in_specs=[in_hbm] * 4,
        out_specs=(pl.BlockSpec(memory_space=pltpu.VMEM),) * 2,
        scratch_shapes=[
            pltpu.VMEM((planes, pad, cols), f32),
            pltpu.VMEM((2, pad, cols), f32),
            pltpu.VMEM((2, pad, cols), f32),
            pltpu.VMEM(plane, jnp.bfloat16),
            pltpu.VMEM(plane, jnp.bfloat16),
            pltpu.VMEM((kl, pad, cols), f32),
            pltpu.VMEM((kl, pad, cols), f32),
            pltpu.VMEM((rows, cols), jnp.int32),
            pltpu.VMEM((3, pad, cols), jnp.bfloat16),
            pltpu.VMEM((5, pad, cols), f32),
            pltpu.VMEM((5, pad, cols), f32),
            pltpu.VMEM((5, ext, cols), f32),
            pltpu.VMEM((5, rows, cols), f32),
            pltpu.VMEM((6, ext, 2 * cols), f32),
            pltpu.VMEM((2, 4 * kl, cols), f32),
            pltpu.VMEM((2, 4 * kl, cols), f32),
            pltpu.VMEM((2, 2 * planes, cols), f32),
            pltpu.VMEM((2, 2 * planes, cols), f32),
            pltpu.VMEM((3, ext, cols), f32),
            pltpu.VMEM((3, ext, cols), f32),
            pltpu.VMEM((ext, cols), f32),
            pltpu.VMEM((ext, cols), f32),
            pltpu.VMEM((ext, cols), f32),
            pltpu.VMEM((2, ext, cols), f32),
            pltpu.VMEM((3, ext, cols), f32),
            pltpu.VMEM((8, cols), f32),
            pltpu.VMEM((gx + gy, 1, cols), f32),
            pltpu.SemaphoreType.DMA((3 + PIECES,)),
            pltpu.SemaphoreType.DMA((4, 8)),
            pltpu.SemaphoreType.DMA((4, 8)),
            pltpu.SemaphoreType.DMA((2, 2)),
            pltpu.SemaphoreType.DMA((2, 2)),
            pltpu.SemaphoreType.DMA((gx + gy,)),
            pltpu.SemaphoreType.DMA((gx + gy,)),
        ],
        compiler_params=pltpu.CompilerParams(
            collective_id=0, has_side_effects=True, vmem_limit_bytes=60 * 1024 * 1024
        ),
    )(tracers.reshape(planes, rows, cols), east_flow, north_flow, levels)
    return new_tracers.reshape(tracers.shape), pressure


def solution(mesh):
    placed = (P(None, None, "gx", "gy"), P(None, "gx", "gy"), P(None, "gx", "gy"), P("gx", "gy"))
    return jax.shard_map(
        functools.partial(on_device, mesh.shape["gx"], mesh.shape["gy"]),
        mesh=mesh,
        in_specs=placed,
        out_specs=(P(None, None, "gx", "gy"), P("gx", "gy")),
        check_vma=False,
    )
```
